128 devices in a mesh: ty: 4 (over z), tx: 32 (over y, x, core).
Axes of the slice: x: 4, y: 4, z: 4, core: 2. Of those that a mesh axis runs over, the one named last changes fastest.
Arguments:
- object_slices: float32 [3, 2, 1024, 8192], P(None, None, 'ty', 'tx'), may hold values from -4 to 4
- window_row: int32 [4, 32, 32], P('ty', 'tx'), may hold values from 0 to 255
- window_column: int32 [4, 32, 32], P('ty', 'tx'), may hold values from 0 to 255
- window_count: int32 [4, 32], P('ty', 'tx'), may hold values from 1 to 32, 256 in all within a row
- intensity: float32 [4, 32, 32, 128, 128], P('ty', 'tx'), may hold values from 0 to 1.5
- probe_wavefield: float32 [2, 128, 128], replicated, may hold values from -5 to 5
Outputs:
- object_grad: float32 [3, 2, 1024, 8192], P(None, None, 'ty', 'tx')
The draws below stay inside these ranges and needn't reach their ends.
Inputs may be any that keep to these rules, and one draw needn't show every extreme that they name: `window_count`: in every row of tiles the counts add up to 256, and some tile of each row holds exactly 32 windows.
All inputs are finite; a program needn't handle non-finite values. No bound on the sum of `window_count` on one device may be relied on, other than what follows from the above.
Results may differ from the reference program's by a relative error of at most 0.0003.
Values sent between devices are 32-bit elements; how exact they have to be, the bound alone decides.
No kernel may reach another device: no remote copies, remote signals or barrier semaphores. Data moves between devices by JAX's collectives and lax.ppermute only.
A program may use at most 192 MiB of HBM per device.

```python
import math
import jax
import jax.numpy as jnp
import numpy as np
from jax import lax

WIN = 128
S = 3
TH = 256
TW = 256
WIN_DEV = 8
CAP = 32
TILE_ROWS = 4
TILE_COLS = 32
NY = 1024
NX = 8192


def set_ends(result, key, least, top_value):
    shape = result.shape
    spot = [jax.random.randint(jax.random.fold_in(key, axis), (), 0, shape[axis]) for axis in range(len(shape))]
    result = result.at[tuple(spot)].set(least)
    longest = shape.index(max(shape))
    spot[longest] = (spot[longest] + 1) % shape[longest]
    return result.at[tuple(spot)].set(top_value)


def block_scale(stream_key, shape, cuts, least, top_value):
    loudness, own = 1.0, jax.random.fold_in(stream_key, 6)
    for position, blocks in cuts:
        steps = jnp.exp(jax.random.uniform(jax.random.fold_in(own, position), (blocks,), jnp.float32, least / len(cuts), top_value / len(cuts)))
        loudness = loudness * jnp.repeat(steps, shape[position] // blocks).reshape([-1 if axis == position else 1 for axis in range(len(shape))])
    return loudness


def split_up(count, total, limit, slope):
    portions = [(1 << 20) // math.isqrt(standing ** slope) + 1 for standing in range(2, count + 1)]
    rest, counts = total - limit - (count - 1), [1] * (count - 1)
    while rest > 0:
        candidates = [i for i in range(count - 1) if counts[i] < limit]
        pool, budget = sum([portions[i] for i in candidates]), rest
        for i in candidates:
            extra = min(limit - counts[i], max(1, budget * portions[i] // pool), rest)
            counts[i] = counts[i] + extra
            rest = rest - extra
    return np.array([limit] + counts)


def ragged(stream_key, amount, total, reach, slope):
    if amount == 2:
        one = jax.random.randint(stream_key, (), max(1, total - reach), min(reach, total - 1) + 1)
        return jnp.stack([one, total - one])
    lengths = jnp.asarray(split_up(amount, total, reach, slope), jnp.int32)
    couples = (amount - 1) // 2
    donor, receiver = lengths[1:1 + 2 * couples:2], lengths[2:2 + 2 * couples:2]
    room = jnp.minimum(donor - 1, reach - receiver)
    passed = jax.random.randint(jax.random.fold_in(stream_key, 1), (couples,), 0, 1 << 20) % (room + 1)
    lengths = lengths.at[1:1 + 2 * couples:2].set(donor - passed).at[2:2 + 2 * couples:2].set(receiver + passed)
    return lengths[jax.random.permutation(jax.random.fold_in(stream_key, 2), amount)]


def scatter_about(rng, shape, spread, most, pieces=(), held_as=jnp.bfloat16):
    gain = block_scale(rng, shape, pieces, -0.22, 0.18) if pieces else 1.0
    result = jax.random.normal(rng, shape, jnp.float32) * spread * gain
    return jnp.minimum(jnp.maximum(result, -most), most).astype(held_as)


def setup_inputs(seed: int = 0) -> dict:
    seeds = jax.random.split(jax.random.key(seed), 7)
    return {
        "object_slices": scatter_about(seeds[0], (S, 2, NY, NX), 0.6, 4.0, ((2, 4), (3, 32)), jnp.float32),
        "window_row": set_ends(jax.random.randint(seeds[1], (TILE_ROWS, TILE_COLS, CAP), 0, TH), jax.random.fold_in(seeds[1], 1), 0, TH - 1).astype(jnp.int32),
        "window_column": set_ends(jax.random.randint(seeds[2], (TILE_ROWS, TILE_COLS, CAP), 0, TW), jax.random.fold_in(seeds[2], 1), 0, TW - 1).astype(jnp.int32),
        "window_count": jax.vmap(lambda own: ragged(own, TILE_COLS, WIN_DEV * TILE_COLS, CAP, 2))(jax.random.split(seeds[3], TILE_ROWS)).reshape((TILE_ROWS, TILE_COLS)).astype(jnp.int32),
        "intensity": jnp.clip(1.5 * jax.random.uniform(seeds[4], (TILE_ROWS, TILE_COLS, CAP, WIN, WIN), jnp.float32) ** block_scale(seeds[4], (TILE_ROWS, TILE_COLS, CAP, WIN, WIN), ((0, 4), (1, 32)), -0.2, 0.2), 0.0, 1.5),
        "probe_wavefield": scatter_about(seeds[5], (2, WIN, WIN), 1.0, 5.0, (), jnp.float32),
    }


propagate_scale = 60.0

def kernel_table(scan_window):
    offsets = jnp.arange(scan_window, dtype=jnp.int32)
    centred = ((offsets + scan_window // 2) % scan_window - scan_window // 2).astype(jnp.float32) / scan_window
    theta = -propagate_scale * (centred[:, None] ** 2 + centred[None, :] ** 2)
    return (jnp.cos(theta), jnp.sin(theta))

def window_loss(patch, measured_intensity, probe_wavefield, kernel):
    field = lax.complex(probe_wavefield[0], probe_wavefield[1])
    for layer_num in range(S):
        field = field * lax.complex(patch[layer_num, 0], patch[layer_num, 1])
        if layer_num + 1 < S:
            field = jnp.fft.ifft2(kernel * jnp.fft.fft2(field, norm='ortho'), norm='ortho')
    far_field = jnp.fft.fft2(field, norm='ortho')
    misfit = jnp.real(far_field) ** 2 + jnp.imag(far_field) ** 2 - measured_intensity
    return 0.5 * jnp.sum(misfit * misfit)

def reference(object_slices, window_row, window_column, window_count, intensity, probe_wavefield):
    kern_re, kern_im = kernel_table(WIN)
    kernel = lax.complex(kern_re, kern_im)
    padded = jnp.pad(object_slices, ((0, 0), (0, 0), (0, WIN), (0, WIN)))
    gradient = jax.grad(window_loss)
    total_slots = TILE_ROWS * TILE_COLS * CAP
    flat_index = jnp.arange(total_slots, dtype=jnp.int32)
    tile_y = flat_index // (TILE_COLS * CAP)
    tile_x = flat_index // CAP % TILE_COLS
    slot_num = flat_index % CAP
    slot_limit = jnp.repeat(window_count.reshape(-1), CAP).astype(jnp.int32)
    records = (tile_y, tile_x, slot_num, window_row.reshape(-1).astype(jnp.int32), window_column.reshape(-1).astype(jnp.int32), slot_limit, intensity.reshape(total_slots, WIN, WIN))

    def step_one(running, record):
        tile_row, tile_col, slot_here, row_off, col_off, limit_here, measured_intensity = record
        anchor = jnp.zeros((), jnp.int32)
        corner_at = (anchor, anchor, (tile_row * TH + row_off).astype(jnp.int32), (tile_col * TW + col_off).astype(jnp.int32))
        patch = lax.dynamic_slice(padded, corner_at, (S, 2, WIN, WIN))
        weight = (slot_here < limit_here).astype(padded.dtype)
        window_grad = gradient(patch, measured_intensity, probe_wavefield, kernel) * weight
        current = lax.dynamic_slice(running, corner_at, (S, 2, WIN, WIN))
        return (lax.dynamic_update_slice(running, current + window_grad, corner_at), None)
    summed = lax.scan(step_one, jnp.zeros_like(padded), records)[0]
    return summed[:, :, :NY, :NX]
```

```python
import functools
import math

import jax
import jax.numpy as jnp
import ml_dtypes
import numpy as np
from jax import lax
from jax.experimental import pallas as pl
from jax.experimental.pallas import tpu as pltpu
from jax.sharding import PartitionSpec as P

WIN = 128
LAYERS = 3
BATCH = 8
PROPAGATE_SCALE = 60.0
F32 = jnp.float32
BF16 = jnp.bfloat16


def complex_tables():
    n = np.arange(WIN)
    dft = np.exp(-2j * math.pi * (n[:, None] * n[None, :] % WIN) / WIN) / math.sqrt(WIN)
    centred = ((n + WIN // 2) % WIN - WIN // 2) / WIN
    phase = np.exp(-1j * PROPAGATE_SCALE * centred**2)
    prop = np.conj(dft) @ (phase[:, None] * dft)
    return prop, dft


def real_form(table):
    return np.block([[table.real, table.imag], [-table.imag, table.real]])


def halves(table):
    high = table.astype(ml_dtypes.bfloat16)
    low = (table - high.astype(np.float64)).astype(ml_dtypes.bfloat16)
    return high, low


def right_table(table):
    high, low = halves(real_form(table))
    return np.concatenate([high, high, low], axis=0)


def left_table(table):
    high, low = halves(real_form(table).T)
    return np.concatenate([high, high, low], axis=1)


def split(x):
    high = x.astype(BF16)
    low = (x - high.astype(F32)).astype(BF16)
    return high, low


def times_right(fields, table):
    rows = jnp.concatenate([jnp.concatenate(f, axis=1) for f in fields], axis=0)
    high, low = split(rows)
    out = jnp.dot(jnp.concatenate([high, low, high], axis=1), table, preferred_element_type=F32)
    return [
        (out[i * WIN : (i + 1) * WIN, :WIN], out[i * WIN : (i + 1) * WIN, WIN:])
        for i in range(len(fields))
    ]


def times_left(fields, table):
    (a_re, a_im), (b_re, b_im) = fields
    cols = jnp.concatenate(
        [jnp.concatenate([a_re, b_re], axis=1), jnp.concatenate([a_im, b_im], axis=1)], axis=0
    )
    high, low = split(cols)
    out = jnp.dot(table, jnp.concatenate([high, low, high], axis=0), preferred_element_type=F32)
    return [(out[:WIN, :WIN], out[WIN:, :WIN]), (out[:WIN, WIN:], out[WIN:, WIN:])]


def both_sides(pairs, right, left):
    return [times_left(times_right(p, right), left) for p in pairs]


def mul(a, b):
    return a[0] * b[0] - a[1] * b[1], a[0] * b[1] + a[1] * b[0]


def mul_conj(a, b):
    return a[0] * b[0] + a[1] * b[1], a[0] * b[1] - a[1] * b[0]


def plan_for(wanted):
    def plan(row, col, used, seen):
        first, second = seen
        inside = jnp.logical_and(used, jnp.logical_and(row <= WIN, col <= WIN))
        above = jnp.logical_and(used, row <= WIN)
        in_first = jnp.logical_and(inside, first < BATCH)
        in_second = jnp.logical_and(
            jnp.logical_and(above, jnp.logical_not(in_first)), second < BATCH
        )
        in_third = jnp.logical_and(used, jnp.logical_not(jnp.logical_or(in_first, in_second)))
        mine = (in_first, in_second, in_third)[wanted]
        return mine, first + in_first.astype(jnp.int32), second + in_second.astype(jnp.int32)

    return plan


def window_kernel(plan, n_in, n_start, ins, starts, outs, *refs):
    row_ref, col_ref, count_ref, intensity_ref, probe_ref, prop_r, prop_l, dft_r, dft_l = refs[:9]
    operands = refs[9 : 9 + n_in + n_start]
    results = refs[9 + n_in + n_start : -9]
    obj, acc, meas, wrapped, order, sem_in, sem_start, sem_meas, sem_out = refs[-9:]
    capacity = intensity_ref.shape[0]

    copies_in = [
        pltpu.make_async_copy(operands[k].at[outer], obj.at[inner], sem_in.at[i])
        for i, (k, outer, inner) in enumerate(ins)
    ]
    copies_start = [
        pltpu.make_async_copy(operands[k].at[outer], acc.at[inner], sem_start.at[i])
        for i, (k, outer, inner) in enumerate(starts[0])
    ]
    for copy in copies_in + copies_start:
        copy.start()

    count = count_ref[0]

    def meas_copy(i):
        return pltpu.make_async_copy(intensity_ref.at[order[i]], meas.at[i], sem_meas.at[i])

    def pick(k, seen):
        n, stage = seen[0], plan(row_ref[k], col_ref[k], k < count, seen[1:])
        mine = stage[0]

        @pl.when(mine)
        def _():
            order[n] = k
            meas_copy(n).start()

        return (n + mine.astype(jnp.int32), *stage[1:])

    zero = jnp.int32(0)
    total = lax.fori_loop(0, capacity, pick, (zero, zero, zero))[0]

    for inner in starts[1]:
        shape = acc.at[inner].shape
        acc[inner] = jnp.zeros(shape, F32)
    for part in range(2):
        wrapped[part, pl.ds(0, 8)] = probe_ref[part, pl.ds(WIN - 8, 8)]
        wrapped[part, pl.ds(8, WIN)] = probe_ref[part]
    for copy in copies_in + copies_start:
        copy.wait()

    lane = lax.broadcasted_iota(jnp.int32, (WIN, WIN), 1)
    head_row = lax.broadcasted_iota(jnp.int32, (8, WIN), 0)

    def step(base, batch):
        def arrived(i, carry):
            meas_copy(i).wait()
            return carry

        lax.fori_loop(base, jnp.minimum(base + batch, total), arrived, 0)
        slots = [base + k for k in range(batch)]
        places = []
        for i in slots:
            k = order[jnp.minimum(i, total - 1)]
            row, col = row_ref[k], col_ref[k]
            top = pl.multiple_of(row // 8 * 8, 8)
            places.append((top, row - top, col // WIN, col % WIN))

        def cut(place, layer):
            top, down, col_tile, shift = place
            here = lane >= shift
            out = []
            for part in range(2):
                plane = layer * 2 + part
                body = jnp.where(
                    here, obj[plane, col_tile, pl.ds(top, WIN)], obj[plane, col_tile + 1, pl.ds(top, WIN)]
                )
                tail = jnp.where(
                    here[:8],
                    obj[plane, col_tile, pl.ds(top + WIN, 8)],
                    obj[plane, col_tile + 1, pl.ds(top + WIN, 8)],
                )
                head = jnp.where(head_row >= down, body[:8], tail)
                out.append(jnp.concatenate([head, body[8:]], axis=0))
            return tuple(out)

        def put(place, layer, grad):
            top, down, col_tile, shift = place
            here = lane >= shift
            for part in range(2):
                plane = layer * 2 + part
                value = grad[part]
                head = jnp.where(head_row >= down, value[:8], 0.0)
                tail = jnp.where(head_row < down, value[:8], 0.0)
                body = jnp.concatenate([head, value[8:]], axis=0)
                acc[plane, col_tile, pl.ds(top, WIN)] += jnp.where(here, body, 0.0)
                acc[plane, col_tile + 1, pl.ds(top, WIN)] += jnp.where(here, 0.0, body)
                acc[plane, col_tile, pl.ds(top + WIN, 8)] += jnp.where(here[:8], tail, 0.0)
                acc[plane, col_tile + 1, pl.ds(top + WIN, 8)] += jnp.where(here[:8], 0.0, tail)

        def through(items, right, left):
            out = []
            for i in range(0, batch, 2):
                out += times_left(times_right(items[i : i + 2], right), left)
            return out

        field = [
            tuple(pltpu.roll(wrapped[part, pl.ds(8 - down, WIN)], shift, 1) for part in range(2))
            for _, down, _, shift in places
        ]
        fields = []
        for layer in range(LAYERS):
            fields.append(field)
            left = [mul(f, cut(p, layer)) for f, p in zip(field, places)]
            if layer + 1 < LAYERS:
                field = through(left, prop_r[...], prop_l[...])
        far = through(left, dft_r[...], dft_l[...])
        grads = []
        for i, (re, im) in zip(slots, far):
            misfit = re * re + im * im - meas[i]
            misfit = jnp.where(i < total, 2.0 * misfit, 0.0)
            grads.append((misfit * re, misfit * im))
        grads = through(grads, inv_right(dft_l), inv_left(dft_r))
        for layer in reversed(range(LAYERS)):
            for place, f, g in zip(places, fields[layer], grads):
                put(place, layer, mul_conj(f, g))
            if layer > 0:
                back = [mul_conj(cut(p, layer), g) for p, g in zip(places, grads)]
                grads = through(back, inv_right(prop_l), inv_left(prop_r))

    small = BATCH // 2
    rest = total % BATCH
    whole = jnp.where(rest > small, total // BATCH + 1, total // BATCH)

    @pl.loop(0, whole)
    def _(it):
        step(it * BATCH, BATCH)

    @pl.when(jnp.logical_and(rest > 0, rest <= small))
    def _():
        step(whole * BATCH, small)

    copies_out = [
        pltpu.make_async_copy(acc.at[inner], results[k].at[outer], sem_out.at[i])
        for i, (k, outer, inner) in enumerate(outs)
    ]
    for copy in copies_out:
        copy.start()
    for copy in copies_out:
        copy.wait()


def inv_right(left_ref):
    high, low = left_ref[:, : 2 * WIN], left_ref[:, 4 * WIN :]
    return jnp.concatenate([high, high, low], axis=0)


def inv_left(right_ref):
    high, low = right_ref[: 2 * WIN], right_ref[4 * WIN :]
    return jnp.concatenate([high, high, low], axis=1)


def per_device(object_slices, window_row, window_column, window_count, intensity, probe_wavefield):
    tile_h, tile_w = object_slices.shape[2:]
    assert tile_h == 2 * WIN and tile_w == 2 * WIN
    capacity = window_row.shape[-1]
    planes = 2 * LAYERS
    tile = object_slices.reshape(planes, tile_h, tile_w)
    rows, cols = lax.axis_size("ty"), lax.axis_size("tx")

    def along(block, axis, distance):
        devices = range(lax.axis_size(axis))
        route = [(i - distance, i) for i in devices if i - distance in devices]
        return lax.ppermute(block, axis, route)

    lower_0 = along(tile[:, :WIN, :WIN], "ty", -1)
    right = along(tile[:, :, :WIN], "tx", -1)
    lower_1 = along(tile[:, :WIN, WIN:], "ty", -1)

    prop, dft = complex_tables()
    tables = [right_table(prop), left_table(prop), right_table(dft), left_table(dft)]
    common = (
        window_row.reshape(capacity),
        window_column.reshape(capacity),
        window_count.reshape(1),
        intensity.reshape(capacity, WIN, WIN),
        probe_wavefield,
        *[jnp.asarray(t) for t in tables],
    )
    smem = pl.BlockSpec(memory_space=pltpu.SMEM)
    hbm = pl.BlockSpec(memory_space=pl.ANY)
    vmem = pl.BlockSpec(memory_space=pltpu.VMEM)
    block = (planes, WIN, WIN)
    everything = slice(None)
    all_rows = pl.ds(0, tile_h)

    def call(name, stage, span, operands, starters, ins, starts, outs, shapes):
        kernel = functools.partial(
            window_kernel, plan_for(stage), len(operands), len(starters), ins, starts, outs
        )
        scratch = (planes, 3, span, WIN)
        return pl.pallas_call(
            kernel,
            out_shape=[jax.ShapeDtypeStruct(s, F32) for s in shapes],
            in_specs=[smem] * 3 + [hbm] + [vmem] * 5 + [hbm] * (len(operands) + len(starters)),
            out_specs=[hbm] * len(shapes),
            scratch_shapes=[
                pltpu.VMEM(scratch, F32),
                pltpu.VMEM(scratch, F32),
                pltpu.VMEM((capacity, WIN, WIN), F32),
                pltpu.VMEM((2, WIN + 8, WIN), F32),
                pltpu.SMEM((capacity,), jnp.int32),
                pltpu.SemaphoreType.DMA((max(1, len(ins)),)),
                pltpu.SemaphoreType.DMA((max(1, len(starts[0])),)),
                pltpu.SemaphoreType.DMA((capacity,)),
                pltpu.SemaphoreType.DMA((len(outs),)),
            ],
            compiler_params=pltpu.CompilerParams(vmem_limit_bytes=48 * 1024 * 1024),
            cost_estimate=pl.CostEstimate(
                flops=1_000_000, bytes_accessed=1_000_000, transcendentals=0
            ),
            name=name,
        )(*common, *operands, *starters)

    def split_cols(k, outer_rows, inner_rows):
        return [
            (k, (everything, outer_rows, pl.ds(t * WIN, WIN)), (everything, t, inner_rows))
            for t in range(2)
        ]

    span = tile_h + 8
    (part,) = call(
        "first_windows",
        0,
        span,
        [tile],
        [],
        split_cols(0, all_rows, all_rows),
        ([], [(everything,)]),
        [(0, (everything,), (everything, everything, all_rows))],
        [(planes, 3, tile_h, WIN)],
    )
    lower_0, _ = lax.optimization_barrier((lower_0, part))
    corner = along(lower_0, "tx", -1)
    (part,) = call(
        "second_windows",
        1,
        span,
        [tile, right, lower_0],
        [part],
        split_cols(0, all_rows, all_rows) + [(1, (everything,), (everything, 2, all_rows))],
        (
            [(3, (everything,), (everything, everything, all_rows))],
            [(everything, everything, pl.ds(tile_h, 8))],
        ),
        [(0, (everything,), (everything, everything, all_rows))],
        [(planes, 3, tile_h, WIN)],
    )
    low = pl.ds(tile_h, WIN)
    main, right_rim, rim_0, rim_1, rim_corner = call(
        "third_windows",
        2,
        tile_h + WIN,
        [tile, right, lower_0, lower_1, corner],
        [part],
        split_cols(0, all_rows, all_rows)
        + [
            (1, (everything,), (everything, 2, all_rows)),
            (2, (everything,), (everything, 0, low)),
            (3, (everything,), (everything, 1, low)),
            (4, (everything,), (everything, 2, low)),
        ],
        (
            [(5, (everything,), (everything, everything, all_rows))],
            [(everything, everything, low)],
        ),
        split_cols(0, all_rows, all_rows)
        + [
            (1, (everything,), (everything, 2, all_rows)),
            (2, (everything,), (everything, 0, low)),
            (3, (everything,), (everything, 1, low)),
            (4, (everything,), (everything, 2, low)),
        ],
        [(planes, tile_h, tile_w), (planes, tile_h, WIN), block, block, block],
    )
    corner_in = along(rim_corner, "tx", 1)
    lower_in_1 = along(rim_1, "ty", 1)
    lower_in_0 = along(rim_0 + corner_in, "ty", 1)
    right_in = along(right_rim, "tx", 1)

    def finish(main_ref, right_ref, low_0_ref, low_1_ref, out_ref):
        out_ref[:, :WIN, :WIN] = main_ref[:, :WIN, :WIN] + (right_ref[:, :WIN] + low_0_ref[...])
        out_ref[:, :WIN, WIN:] = main_ref[:, :WIN, WIN:] + low_1_ref[...]
        out_ref[:, WIN:, :WIN] = main_ref[:, WIN:, :WIN] + right_ref[:, WIN:]
        out_ref[:, WIN:, WIN:] = main_ref[:, WIN:, WIN:]

    step = 3
    per_plane = lambda *s: pl.BlockSpec((step, *s), lambda p: (p, 0, 0))
    out = pl.pallas_call(
        finish,
        grid=(planes // step,),
        out_shape=jax.ShapeDtypeStruct((planes, tile_h, tile_w), F32),
        in_specs=[
            per_plane(tile_h, tile_w),
            per_plane(tile_h, WIN),
            per_plane(WIN, WIN),
            per_plane(WIN, WIN),
        ],
        out_specs=per_plane(tile_h, tile_w),
        name="add_rims",
    )(main, right_in, lower_in_0, lower_in_1)
    return out.reshape(object_slices.shape)


def solution(mesh):
    return jax.shard_map(
        per_device,
        mesh=mesh,
        in_specs=(
            P(None, None, "ty", "tx"),
            P("ty", "tx", None),
            P("ty", "tx", None),
            P("ty", "tx"),
            P("ty", "tx", None, None, None),
            P(),
        ),
        out_specs=P(None, None, "ty", "tx"),
        check_vma=False,
    )
```

```python
import functools
import math

import jax
import jax.numpy as jnp
import ml_dtypes
import numpy as np
from jax import lax
from jax.experimental import pallas as pl
from jax.experimental.pallas import tpu as pltpu
from jax.sharding import PartitionSpec as P

WIN = 128
LAYERS = 3
BATCH = 8
PROPAGATE_SCALE = 60.0
F32 = jnp.float32
BF16 = jnp.bfloat16


def complex_tables():
    n = np.arange(WIN)
    dft = np.exp(-2j * math.pi * (n[:, None] * n[None, :] % WIN) / WIN) / math.sqrt(WIN)
    centred = ((n + WIN // 2) % WIN - WIN // 2) / WIN
    phase = np.exp(-1j * PROPAGATE_SCALE * centred**2)
    prop = np.conj(dft) @ (phase[:, None] * dft)
    return prop, dft


def real_form(table):
    return np.block([[table.real, table.imag], [-table.imag, table.real]])


def halves(table):
    high = table.astype(ml_dtypes.bfloat16)
    low = (table - high.astype(np.float64)).astype(ml_dtypes.bfloat16)
    return high, low


def right_table(table):
    high, low = halves(real_form(table))
    return np.concatenate([high, high, low], axis=0)


def left_table(table):
    high, low = halves(real_form(table).T)
    return np.concatenate([high, high, low], axis=1)


def split(x):
    high = x.astype(BF16)
    low = (x - high.astype(F32)).astype(BF16)
    return high, low


def times_right(fields, table):
    rows = jnp.concatenate([jnp.concatenate(f, axis=1) for f in fields], axis=0)
    high, low = split(rows)
    out = jnp.dot(jnp.concatenate([high, low, high], axis=1), table, preferred_element_type=F32)
    return [
        (out[i * WIN : (i + 1) * WIN, :WIN], out[i * WIN : (i + 1) * WIN, WIN:])
        for i in range(len(fields))
    ]


def times_left(fields, table):
    (a_re, a_im), (b_re, b_im) = fields
    cols = jnp.concatenate(
        [jnp.concatenate([a_re, b_re], axis=1), jnp.concatenate([a_im, b_im], axis=1)], axis=0
    )
    high, low = split(cols)
    out = jnp.dot(table, jnp.concatenate([high, low, high], axis=0), preferred_element_type=F32)
    return [(out[:WIN, :WIN], out[WIN:, :WIN]), (out[:WIN, WIN:], out[WIN:, WIN:])]


def both_sides(pairs, right, left):
    return [times_left(times_right(p, right), left) for p in pairs]


def mul(a, b):
    return a[0] * b[0] - a[1] * b[1], a[0] * b[1] + a[1] * b[0]


def mul_conj(a, b):
    return a[0] * b[0] + a[1] * b[1], a[0] * b[1] - a[1] * b[0]


def plan_for(wanted):
    def plan(row, col, used, seen):
        first, second = seen
        inside = jnp.logical_and(used, jnp.logical_and(row <= WIN, col <= WIN))
        above = jnp.logical_and(used, row <= WIN)
        in_first = jnp.logical_and(inside, first < BATCH)
        in_second = jnp.logical_and(
            jnp.logical_and(above, jnp.logical_not(in_first)), second < BATCH
        )
        in_third = jnp.logical_and(used, jnp.logical_not(jnp.logical_or(in_first, in_second)))
        mine = (in_first, in_second, in_third)[wanted]
        return mine, first + in_first.astype(jnp.int32), second + in_second.astype(jnp.int32)

    return plan


def window_kernel(plan, ins, n_in, carried, rims, *refs):
    row_ref, col_ref, count_ref, meas, probe_ref, prop_r, prop_l, dft_r, dft_l = refs[:9]
    operands = refs[9 : 9 + n_in]
    acc, *results = refs[9 + n_in + carried : -3]
    obj, wrapped, order = refs[-3:]
    capacity = meas.shape[0]
    count = count_ref[0]

    def pick(k, seen):
        n, stage = seen[0], plan(row_ref[k], col_ref[k], k < count, seen[1:])
        order[n] = k
        return (n + stage[0].astype(jnp.int32), *stage[1:])

    zero = jnp.int32(0)
    total = lax.fori_loop(0, count, pick, (zero, zero, zero))[0]

    if carried:
        acc[...] = refs[9 + n_in][...]
    else:
        acc[...] = jnp.zeros(acc.shape, F32)
    for k, outer, inner in ins:
        obj[inner] = operands[k][outer]
    for part in range(2):
        wrapped[part, pl.ds(0, 8)] = probe_ref[part, pl.ds(WIN - 8, 8)]
        wrapped[part, pl.ds(8, WIN)] = probe_ref[part]

    lane = lax.broadcasted_iota(jnp.int32, (WIN, WIN), 1)
    head_row = lax.broadcasted_iota(jnp.int32, (8, WIN), 0)

    def step(base, batch):
        slots = [order[jnp.minimum(base + k, total - 1)] for k in range(batch)]
        places = []
        for k in slots:
            row, col = row_ref[k], col_ref[k]
            top = pl.multiple_of(row // 8 * 8, 8)
            places.append((top, row - top, col // WIN, col % WIN))

        def cut(place, layer):
            top, down, col_tile, shift = place
            here = lane >= shift
            out = []
            for part in range(2):
                plane = layer * 2 + part
                body = jnp.where(
                    here, obj[plane, col_tile, pl.ds(top, WIN)], obj[plane, col_tile + 1, pl.ds(top, WIN)]
                )
                tail = jnp.where(
                    here[:8],
                    obj[plane, col_tile, pl.ds(top + WIN, 8)],
                    obj[plane, col_tile + 1, pl.ds(top + WIN, 8)],
                )
                head = jnp.where(head_row >= down, body[:8], tail)
                out.append(jnp.concatenate([head, body[8:]], axis=0))
            return tuple(out)

        def put(place, layer, grad):
            top, down, col_tile, shift = place
            here = lane >= shift
            for part in range(2):
                plane = layer * 2 + part
                value = grad[part]
                head = jnp.where(head_row >= down, value[:8], 0.0)
                tail = jnp.where(head_row < down, value[:8], 0.0)
                body = jnp.concatenate([head, value[8:]], axis=0)
                acc[plane, col_tile, pl.ds(top, WIN)] += jnp.where(here, body, 0.0)
                acc[plane, col_tile + 1, pl.ds(top, WIN)] += jnp.where(here, 0.0, body)
                acc[plane, col_tile, pl.ds(top + WIN, 8)] += jnp.where(here[:8], tail, 0.0)
                acc[plane, col_tile + 1, pl.ds(top + WIN, 8)] += jnp.where(here[:8], 0.0, tail)

        def through(items, right, left):
            out = []
            for i in range(0, batch, 2):
                out += times_left(times_right(items[i : i + 2], right), left)
            return out

        field = [
            tuple(pltpu.roll(wrapped[part, pl.ds(8 - down, WIN)], shift, 1) for part in range(2))
            for _, down, _, shift in places
        ]
        fields = []
        for layer in range(LAYERS):
            fields.append(field)
            left = [mul(f, cut(p, layer)) for f, p in zip(field, places)]
            if layer + 1 < LAYERS:
                field = through(left, prop_r[...], prop_l[...])
        far = through(left, dft_r[...], dft_l[...])
        grads = []
        for i, (k, (re, im)) in enumerate(zip(slots, far)):
            misfit = re * re + im * im - meas[k]
            misfit = jnp.where(base + i < total, 2.0 * misfit, 0.0)
            grads.append((misfit * re, misfit * im))
        grads = through(grads, inv_right(dft_l), inv_left(dft_r))
        for layer in reversed(range(LAYERS)):
            for place, f, g in zip(places, fields[layer], grads):
                put(place, layer, mul_conj(f, g))
            if layer > 0:
                back = [mul_conj(cut(p, layer), g) for p, g in zip(places, grads)]
                grads = through(back, inv_right(prop_l), inv_left(prop_r))

    small = BATCH // 2
    rest = total % BATCH
    whole = jnp.where(rest > small, total // BATCH + 1, total // BATCH)

    @pl.loop(0, whole)
    def _(it):
        step(it * BATCH, BATCH)

    @pl.when(jnp.logical_and(rest > 0, rest <= small))
    def _():
        step(whole * BATCH, small)

    for k, outer, inner in rims:
        results[k][outer] = acc[inner]


def inv_right(left_ref):
    high, low = left_ref[:, : 2 * WIN], left_ref[:, 4 * WIN :]
    return jnp.concatenate([high, high, low], axis=0)


def inv_left(right_ref):
    high, low = right_ref[: 2 * WIN], right_ref[4 * WIN :]
    return jnp.concatenate([high, high, low], axis=1)


def per_device(object_slices, window_row, window_column, window_count, intensity, probe_wavefield):
    tile_h, tile_w = object_slices.shape[2:]
    assert tile_h == 2 * WIN and tile_w == 2 * WIN
    capacity = window_row.shape[-1]
    planes = 2 * LAYERS
    tile = object_slices.reshape(planes, tile_h, tile_w)
    rows, cols = lax.axis_size("ty"), lax.axis_size("tx")

    def along(block, axis, distance):
        devices = range(lax.axis_size(axis))
        route = [(i - distance, i) for i in devices if i - distance in devices]
        return lax.ppermute(block, axis, route)

    lower_0 = along(tile[:, :WIN, :WIN], "ty", -1)
    right = along(tile[:, :, :WIN], "tx", -1)
    lower_1 = along(tile[:, :WIN, WIN:], "ty", -1)

    prop, dft = complex_tables()
    tables = [right_table(prop), left_table(prop), right_table(dft), left_table(dft)]
    common = (
        window_row.reshape(capacity),
        window_column.reshape(capacity),
        window_count.reshape(1),
        intensity.reshape(capacity, WIN, WIN),
        probe_wavefield,
        *[jnp.asarray(t) for t in tables],
    )
    smem = pl.BlockSpec(memory_space=pltpu.SMEM)
    hbm = pl.BlockSpec(memory_space=pl.ANY)
    vmem = pl.BlockSpec(memory_space=pltpu.VMEM)
    block = (planes, WIN, WIN)
    everything = slice(None)
    high, low = slice(0, tile_h), slice(tile_h, tile_h + WIN)
    whole = (planes, 3, tile_h + WIN, WIN)

    def call(name, stage, operands, carried, ins, rims, shapes):
        kernel = functools.partial(
            window_kernel, plan_for(stage), ins, len(operands), len(carried), rims
        )
        return pl.pallas_call(
            kernel,
            out_shape=[jax.ShapeDtypeStruct(s, F32) for s in (whole, *shapes)],
            in_specs=[smem] * 3 + [vmem] * (6 + len(operands) + len(carried)),
            out_specs=[vmem] * (1 + len(shapes)),
            scratch_shapes=[
                pltpu.VMEM(whole, F32),
                pltpu.VMEM((2, WIN + 8, WIN), F32),
                pltpu.SMEM((capacity + 1,), jnp.int32),
            ],
            compiler_params=pltpu.CompilerParams(vmem_limit_bytes=32 * 1024 * 1024),
            cost_estimate=pl.CostEstimate(
                flops=1_000_000, bytes_accessed=1_000_000, transcendentals=0
            ),
            name=name,
        )(*common, *operands, *carried)

    def split_cols(k):
        return [
            (k, (everything, everything, slice(t * WIN, (t + 1) * WIN)), (everything, t, high))
            for t in range(2)
        ]

    (part,) = call("first_windows", 0, [tile], [], split_cols(0), [], [])
    lower_0, _ = lax.optimization_barrier((lower_0, part))
    corner = along(lower_0, "tx", -1)
    with_right = split_cols(0) + [(1, (everything,), (everything, 2, high))]
    (part,) = call("second_windows", 1, [tile, right, lower_0], [part], with_right, [], [])
    main, *right_rims, rim_0, rim_1, rim_corner = call(
        "third_windows",
        2,
        [tile, right, lower_0, lower_1, corner],
        [part],
        with_right + [(2 + t, (everything,), (everything, t, low)) for t in range(3)],
        [(i, (everything,), (slice(2 * i, 2 * i + 2), 2, high)) for i in range(LAYERS)]
        + [(LAYERS + t, (everything,), (everything, t, low)) for t in range(3)],
        [(2, tile_h, WIN)] * LAYERS + [block] * 3,
    )
    corner_in = along(rim_corner, "tx", 1)
    lower_in_1 = along(rim_1, "ty", 1)
    lower_in_0 = along(rim_0 + corner_in, "ty", 1)
    right_in = [along(rim, "tx", 1) for rim in right_rims]

    def finish(main_ref, *refs):
        *rights, low_0_ref, low_1_ref, out_ref, out, sems = refs
        copies = []
        for p in range(planes):
            right_ref = rights[p // 2]
            out[p, :WIN, :WIN] = main_ref[p, 0, :WIN] + (right_ref[p % 2, :WIN] + low_0_ref[p])
            out[p, :WIN, WIN:] = main_ref[p, 1, :WIN] + low_1_ref[p]
            out[p, WIN:, :WIN] = main_ref[p, 0, WIN:tile_h] + right_ref[p % 2, WIN:]
            out[p, WIN:, WIN:] = main_ref[p, 1, WIN:tile_h]
            copies.append(pltpu.make_async_copy(out.at[p], out_ref.at[p], sems.at[p]))
            copies[-1].start()
        for copy in copies:
            copy.wait()

    out = pl.pallas_call(
        finish,
        out_shape=jax.ShapeDtypeStruct((planes, tile_h, tile_w), F32),
        in_specs=[vmem] * (3 + LAYERS),
        out_specs=hbm,
        scratch_shapes=[
            pltpu.VMEM((planes, tile_h, tile_w), F32),
            pltpu.SemaphoreType.DMA((planes,)),
        ],
        compiler_params=pltpu.CompilerParams(vmem_limit_bytes=16 * 1024 * 1024),
        name="add_rims",
    )(main, *right_in, lower_in_0, lower_in_1)
    return out.reshape(object_slices.shape)


def solution(mesh):
    return jax.shard_map(
        per_device,
        mesh=mesh,
        in_specs=(
            P(None, None, "ty", "tx"),
            P("ty", "tx", None),
            P("ty", "tx", None),
            P("ty", "tx"),
            P("ty", "tx", None, None, None),
            P(),
        ),
        out_specs=P(None, None, "ty", "tx"),
        check_vma=False,
    )
```

```python
import functools
import math

import jax
import jax.numpy as jnp
import ml_dtypes
import numpy as np
from jax import lax
from jax.experimental import pallas as pl
from jax.experimental.pallas import tpu as pltpu
from jax.sharding import PartitionSpec as P

WIN = 128
LAYERS = 3
BATCH = 8
PROP, DFT = 0, 4
PROPAGATE_SCALE = 60.0
F32 = jnp.float32
BF16 = jnp.bfloat16


def complex_tables():
    n = np.arange(WIN)
    dft = np.exp(-2j * math.pi * (n[:, None] * n[None, :] % WIN) / WIN) / math.sqrt(WIN)
    centred = ((n + WIN // 2) % WIN - WIN // 2) / WIN
    phase = np.exp(-1j * PROPAGATE_SCALE * centred**2)
    prop = np.conj(dft) @ (phase[:, None] * dft)
    return prop, dft


def real_form(table):
    return np.block([[table.real, table.imag], [-table.imag, table.real]])


def halves(table):
    high = table.astype(ml_dtypes.bfloat16)
    low = (table - high.astype(np.float64)).astype(ml_dtypes.bfloat16)
    return high, low


def table_blocks():
    blocks = []
    for table in complex_tables():
        for form in (real_form(table), real_form(table).T):
            blocks += halves(form)
    return np.stack(blocks)


def right_table(tables, which):
    high, low = tables[which], tables[which + 1]
    return jnp.concatenate([high, high, low], axis=0)


def left_table(tables, which):
    high, low = tables[which], tables[which + 1]
    return jnp.concatenate([high, high, low], axis=1)


def split(x):
    high = x.astype(BF16)
    low = (x - high.astype(F32)).astype(BF16)
    return high, low


def times_right(fields, table):
    rows = jnp.concatenate([jnp.concatenate(f, axis=1) for f in fields], axis=0)
    high, low = split(rows)
    out = jnp.dot(jnp.concatenate([high, low, high], axis=1), table, preferred_element_type=F32)
    return [
        (out[i * WIN : (i + 1) * WIN, :WIN], out[i * WIN : (i + 1) * WIN, WIN:])
        for i in range(len(fields))
    ]


def times_left(fields, table):
    (a_re, a_im), (b_re, b_im) = fields
    cols = jnp.concatenate(
        [jnp.concatenate([a_re, b_re], axis=1), jnp.concatenate([a_im, b_im], axis=1)], axis=0
    )
    high, low = split(cols)
    out = jnp.dot(table, jnp.concatenate([high, low, high], axis=0), preferred_element_type=F32)
    return [(out[:WIN, :WIN], out[WIN:, :WIN]), (out[:WIN, WIN:], out[WIN:, WIN:])]


def both_sides(pairs, right, left):
    return [times_left(times_right(p, right), left) for p in pairs]


def mul(a, b):
    return a[0] * b[0] - a[1] * b[1], a[0] * b[1] + a[1] * b[0]


def mul_conj(a, b):
    return a[0] * b[0] + a[1] * b[1], a[0] * b[1] - a[1] * b[0]


def plan_for(wanted, row_ref, col_ref, count):
    zero = jnp.int32(0)
    one = lambda flag: flag.astype(jnp.int32)

    def kind(k):
        low, far = row_ref[k] > WIN, col_ref[k] > WIN
        high, near = jnp.logical_not(low), jnp.logical_not(far)
        return (
            jnp.logical_and(high, near),
            jnp.logical_and(high, far),
            jnp.logical_and(low, far),
        )

    def tally(k, seen):
        return tuple(n + one(flag) for n, flag in zip(seen, kind(k)))

    n_inside_all, n_right, n_corner = lax.fori_loop(0, count, tally, (zero, zero, zero))
    small = BATCH // 2
    fill_1 = BATCH + jnp.maximum(BATCH - n_right, 0)
    n_late = n_corner + jnp.maximum(n_right - BATCH, 0)
    fill_2 = (n_late + small - 1) // small * small - n_late
    n_early = jnp.minimum(n_right, BATCH) + jnp.minimum(n_inside_all, fill_1)
    fill_2 = jnp.where(count - n_early <= BATCH + small, count, fill_2)

    def stage(k, seen):
        n_inside, n_right, n_pool = seen
        inside, right, corner = kind(k)
        first = jnp.logical_and(inside, n_inside < BATCH)
        second = jnp.logical_or(
            jnp.logical_and(right, n_right < BATCH),
            jnp.logical_and(inside, jnp.logical_and(n_inside >= BATCH, n_inside < fill_1)),
        )
        third = jnp.logical_or(corner, jnp.logical_and(right, n_right >= BATCH))
        pool = jnp.logical_not(jnp.logical_or(first, jnp.logical_or(second, third)))
        fills = jnp.logical_and(pool, n_pool < fill_2)
        mine = (
            first,
            second,
            jnp.logical_or(third, fills),
            jnp.logical_and(pool, n_pool >= fill_2),
        )[wanted]
        return mine, n_inside + one(inside), n_right + one(right), n_pool + one(pool)

    return stage


def window_kernel(wanted, ins, n_in, carried, rims, *refs):
    row_ref, col_ref, count_ref, meas, probe_ref, tables = refs[:6]
    operands = refs[6 : 6 + n_in]
    acc, *results = refs[6 + n_in + carried : -3]
    obj, wrapped, order = refs[-3:]
    capacity = meas.shape[0]
    count = count_ref[0]

    stage = plan_for(wanted, row_ref, col_ref, count)

    def pick(k, seen):
        n = seen[0]
        mine, *later = stage(k, seen[1:])
        order[n] = k
        return (n + mine.astype(jnp.int32), *later)

    zero = jnp.int32(0)
    total = lax.fori_loop(0, count, pick, (zero, zero, zero, zero))[0]

    if carried:
        acc[...] = refs[6 + n_in][...]
    else:
        acc[...] = jnp.zeros(acc.shape, F32)
    for k, outer, inner in ins:
        obj[inner] = operands[k][outer]
    for part in range(2):
        wrapped[part, pl.ds(0, 8)] = probe_ref[part, pl.ds(WIN - 8, 8)]
        wrapped[part, pl.ds(8, WIN)] = probe_ref[part]

    lane = lax.broadcasted_iota(jnp.int32, (WIN, WIN), 1)
    head_row = lax.broadcasted_iota(jnp.int32, (8, WIN), 0)

    def step(base, batch):
        slots = [order[jnp.minimum(base + k, total - 1)] for k in range(batch)]
        places = []
        for k in slots:
            row, col = row_ref[k], col_ref[k]
            top = pl.multiple_of(row // 8 * 8, 8)
            places.append((top, row - top, col // WIN, col % WIN))

        def cut(place, layer):
            top, down, col_tile, shift = place
            here = lane >= shift
            out = []
            for part in range(2):
                plane = layer * 2 + part
                body = jnp.where(
                    here, obj[plane, col_tile, pl.ds(top, WIN)], obj[plane, col_tile + 1, pl.ds(top, WIN)]
                )
                tail = jnp.where(
                    here[:8],
                    obj[plane, col_tile, pl.ds(top + WIN, 8)],
                    obj[plane, col_tile + 1, pl.ds(top + WIN, 8)],
                )
                head = jnp.where(head_row >= down, body[:8], tail)
                out.append(jnp.concatenate([head, body[8:]], axis=0))
            return tuple(out)

        def put(place, layer, grad):
            top, down, col_tile, shift = place
            here = lane >= shift
            for part in range(2):
                plane = layer * 2 + part
                value = grad[part]
                head = jnp.where(head_row >= down, value[:8], 0.0)
                tail = jnp.where(head_row < down, value[:8], 0.0)
                body = jnp.concatenate([head, value[8:]], axis=0)
                acc[plane, col_tile, pl.ds(top, WIN)] += jnp.where(here, body, 0.0)
                acc[plane, col_tile + 1, pl.ds(top, WIN)] += jnp.where(here, 0.0, body)
                acc[plane, col_tile, pl.ds(top + WIN, 8)] += jnp.where(here[:8], tail, 0.0)
                acc[plane, col_tile + 1, pl.ds(top + WIN, 8)] += jnp.where(here[:8], 0.0, tail)

        def through(items, right, left):
            out = []
            for i in range(0, batch, 2):
                out += times_left(
                    times_right(items[i : i + 2], right_table(tables, right)),
                    left_table(tables, left),
                )
            return out

        field = [
            tuple(pltpu.roll(wrapped[part, pl.ds(8 - down, WIN)], shift, 1) for part in range(2))
            for _, down, _, shift in places
        ]
        fields = []
        for layer in range(LAYERS):
            fields.append(field)
            left = [mul(f, cut(p, layer)) for f, p in zip(field, places)]
            if layer + 1 < LAYERS:
                field = through(left, PROP, PROP + 2)
        far = through(left, DFT, DFT + 2)
        grads = []
        for i, (k, (re, im)) in enumerate(zip(slots, far)):
            misfit = re * re + im * im - meas[k]
            misfit = jnp.where(base + i < total, 2.0 * misfit, 0.0)
            grads.append((misfit * re, misfit * im))
        grads = through(grads, DFT + 2, DFT)
        for layer in reversed(range(LAYERS)):
            for place, f, g in zip(places, fields[layer], grads):
                put(place, layer, mul_conj(f, g))
            if layer > 0:
                back = [mul_conj(cut(p, layer), g) for p, g in zip(places, grads)]
                grads = through(back, PROP + 2, PROP)

    small = BATCH // 2
    rest = total % BATCH
    whole = jnp.where(rest > small, total // BATCH + 1, total // BATCH)

    @pl.loop(0, whole)
    def _(it):
        step(it * BATCH, BATCH)

    @pl.when(jnp.logical_and(rest > 0, rest <= small))
    def _():
        step(whole * BATCH, small)

    for k, outer, inner in rims:
        results[k][outer] = acc[inner]


def per_device(object_slices, window_row, window_column, window_count, intensity, probe_wavefield):
    tile_h, tile_w = object_slices.shape[2:]
    assert tile_h == 2 * WIN and tile_w == 2 * WIN
    capacity = window_row.shape[-1]
    planes = 2 * LAYERS
    tile = object_slices.reshape(planes, tile_h, tile_w)
    rows, cols = lax.axis_size("ty"), lax.axis_size("tx")

    def along(block, axis, distance):
        devices = range(lax.axis_size(axis))
        route = [(i - distance, i) for i in devices if i - distance in devices]
        return lax.ppermute(block, axis, route)

    lower_0 = along(tile[:, :WIN, :WIN], "ty", -1)
    right = along(tile[:, :, :WIN], "tx", -1)
    lower_1 = along(tile[:, :WIN, WIN:], "ty", -1)

    common = (
        window_row.reshape(capacity),
        window_column.reshape(capacity),
        window_count.reshape(1),
        intensity.reshape(capacity, WIN, WIN),
        probe_wavefield,
        jnp.asarray(table_blocks()),
    )
    smem = pl.BlockSpec(memory_space=pltpu.SMEM)
    hbm = pl.BlockSpec(memory_space=pl.ANY)
    vmem = pl.BlockSpec(memory_space=pltpu.VMEM)
    block = (planes, WIN, WIN)
    everything = slice(None)
    high, low = slice(0, tile_h), slice(tile_h, tile_h + WIN)
    whole = (planes, 3, tile_h + WIN, WIN)

    def call(name, stage, operands, carried, ins, rims, shapes):
        kernel = functools.partial(
            window_kernel, stage, ins, len(operands), len(carried), rims
        )
        return pl.pallas_call(
            kernel,
            out_shape=[jax.ShapeDtypeStruct(s, F32) for s in (whole, *shapes)],
            in_specs=[smem] * 3 + [vmem] * (3 + len(operands) + len(carried)),
            out_specs=[vmem] * (1 + len(shapes)),
            scratch_shapes=[
                pltpu.VMEM(whole, F32),
                pltpu.VMEM((2, WIN + 8, WIN), F32),
                pltpu.SMEM((capacity + 1,), jnp.int32),
            ],
            compiler_params=pltpu.CompilerParams(vmem_limit_bytes=32 * 1024 * 1024),
            cost_estimate=pl.CostEstimate(
                flops=1_000_000, bytes_accessed=1_000_000, transcendentals=0
            ),
            name=name,
        )(*common, *operands, *carried)

    def split_cols(k):
        return [
            (k, (everything, everything, slice(t * WIN, (t + 1) * WIN)), (everything, t, high))
            for t in range(2)
        ]

    (part,) = call("inside_windows", 0, [tile], [], split_cols(0), [], [])
    lower_0, _ = lax.optimization_barrier((lower_0, part))
    corner = along(lower_0, "tx", -1)
    with_right = split_cols(0) + [(1, (everything,), (everything, 2, high))]
    (part,) = call("right_windows", 1, [tile, right, lower_0], [part], with_right, [], [])
    with_all = with_right + [(2 + t, (everything,), (everything, t, low)) for t in range(3)]
    strips = [tile, right, lower_0, lower_1, corner]
    part, right_rim, rim_corner = call(
        "corner_windows",
        2,
        strips,
        [part],
        with_all,
        [(0, (everything,), (everything, 2, high)), (1, (everything,), (everything, 2, low))],
        [(planes, tile_h, WIN), block],
    )
    corner_in = along(rim_corner, "tx", 1)
    right_in = along(right_rim, "tx", 1)
    main, rim_0, rim_1 = call(
        "lower_windows",
        3,
        strips,
        [part],
        with_all,
        [(t, (everything,), (everything, t, low)) for t in range(2)],
        [block] * 2,
    )
    lower_in_1 = along(rim_1, "ty", 1)
    lower_in_0 = along(rim_0 + corner_in, "ty", 1)

    def finish(main_ref, right_ref, low_0_ref, low_1_ref, out_ref, out, sems):
        copies = []
        for p in range(planes):
            out[p, :WIN, :WIN] = main_ref[p, 0, :WIN] + (right_ref[p, :WIN] + low_0_ref[p])
            out[p, :WIN, WIN:] = main_ref[p, 1, :WIN] + low_1_ref[p]
            out[p, WIN:, :WIN] = main_ref[p, 0, WIN:tile_h] + right_ref[p, WIN:]
            out[p, WIN:, WIN:] = main_ref[p, 1, WIN:tile_h]
            copies.append(pltpu.make_async_copy(out.at[p], out_ref.at[p], sems.at[p]))
            copies[-1].start()
        for copy in copies:
            copy.wait()

    out = pl.pallas_call(
        finish,
        out_shape=jax.ShapeDtypeStruct((planes, tile_h, tile_w), F32),
        in_specs=[vmem] * 4,
        out_specs=hbm,
        scratch_shapes=[
            pltpu.VMEM((planes, tile_h, tile_w), F32),
            pltpu.SemaphoreType.DMA((planes,)),
        ],
        compiler_params=pltpu.CompilerParams(vmem_limit_bytes=16 * 1024 * 1024),
        name="add_rims",
    )(main, right_in, lower_in_0, lower_in_1)
    return out.reshape(object_slices.shape)


def solution(mesh):
    return jax.shard_map(
        per_device,
        mesh=mesh,
        in_specs=(
            P(None, None, "ty", "tx"),
            P("ty", "tx", None),
            P("ty", "tx", None),
            P("ty", "tx"),
            P("ty", "tx", None, None, None),
            P(),
        ),
        out_specs=P(None, None, "ty", "tx"),
        check_vma=False,
    )
```

```python
import functools
import math

import jax
import jax.numpy as jnp
import ml_dtypes
import numpy as np
from jax import lax
from jax.experimental import pallas as pl
from jax.experimental.pallas import tpu as pltpu
from jax.sharding import PartitionSpec as P

WIN = 128
LAYERS = 3
BATCH = 8
PROP, DFT = 0, 4
PROPAGATE_SCALE = 60.0
F32 = jnp.float32
BF16 = jnp.bfloat16


def complex_tables():
    n = np.arange(WIN)
    dft = np.exp(-2j * math.pi * (n[:, None] * n[None, :] % WIN) / WIN) / math.sqrt(WIN)
    centred = ((n + WIN // 2) % WIN - WIN // 2) / WIN
    phase = np.exp(-1j * PROPAGATE_SCALE * centred**2)
    prop = np.conj(dft) @ (phase[:, None] * dft)
    return prop, dft


def real_form(table):
    return np.block([[table.real, table.imag], [-table.imag, table.real]])


def halves(table):
    high = table.astype(ml_dtypes.bfloat16)
    low = (table - high.astype(np.float64)).astype(ml_dtypes.bfloat16)
    return high, low


def table_blocks():
    blocks = []
    for table in complex_tables():
        for form in (real_form(table), real_form(table).T):
            blocks += halves(form)
    return np.stack(blocks)


def right_table(tables, which):
    high, low = tables[which], tables[which + 1]
    return jnp.concatenate([high, high, low], axis=0)


def left_table(tables, which):
    high, low = tables[which], tables[which + 1]
    return jnp.concatenate([high, high, low], axis=1)


def split(x):
    high = x.astype(BF16)
    low = (x - high.astype(F32)).astype(BF16)
    return high, low


def times_right(fields, table):
    rows = jnp.concatenate([jnp.concatenate(f, axis=1) for f in fields], axis=0)
    high, low = split(rows)
    out = jnp.dot(jnp.concatenate([high, low, high], axis=1), table, preferred_element_type=F32)
    return [
        (out[i * WIN : (i + 1) * WIN, :WIN], out[i * WIN : (i + 1) * WIN, WIN:])
        for i in range(len(fields))
    ]


def times_left(fields, table):
    (a_re, a_im), (b_re, b_im) = fields
    cols = jnp.concatenate(
        [jnp.concatenate([a_re, b_re], axis=1), jnp.concatenate([a_im, b_im], axis=1)], axis=0
    )
    high, low = split(cols)
    out = jnp.dot(table, jnp.concatenate([high, low, high], axis=0), preferred_element_type=F32)
    return [(out[:WIN, :WIN], out[WIN:, :WIN]), (out[:WIN, WIN:], out[WIN:, WIN:])]


def both_sides(pairs, right, left):
    return [times_left(times_right(p, right), left) for p in pairs]


def mul(a, b):
    return a[0] * b[0] - a[1] * b[1], a[0] * b[1] + a[1] * b[0]


def mul_conj(a, b):
    return a[0] * b[0] + a[1] * b[1], a[0] * b[1] - a[1] * b[0]


def plan_for(wanted, row_ref, col_ref, count):
    zero = jnp.int32(0)
    one = lambda flag: flag.astype(jnp.int32)

    def kind(k):
        low, far = row_ref[k] > WIN, col_ref[k] > WIN
        high, near = jnp.logical_not(low), jnp.logical_not(far)
        return (
            jnp.logical_and(high, near),
            jnp.logical_and(high, far),
            jnp.logical_and(low, far),
        )

    def tally(k, seen):
        return tuple(n + one(flag) for n, flag in zip(seen, kind(k)))

    n_inside_all, n_right, n_corner = lax.fori_loop(0, count, tally, (zero, zero, zero))
    small = BATCH // 2
    fill_1 = BATCH + jnp.maximum(BATCH - n_right, 0)
    n_late = n_corner + jnp.maximum(n_right - BATCH, 0)
    fill_2 = (n_late + small - 1) // small * small - n_late
    n_early = jnp.minimum(n_right, BATCH) + jnp.minimum(n_inside_all, fill_1)
    fill_2 = jnp.where(count - n_early <= BATCH + small, count, fill_2)

    def stage(k, seen):
        n_inside, n_right, n_pool = seen
        inside, right, corner = kind(k)
        first = jnp.logical_and(inside, n_inside < BATCH)
        second = jnp.logical_or(
            jnp.logical_and(right, n_right < BATCH),
            jnp.logical_and(inside, jnp.logical_and(n_inside >= BATCH, n_inside < fill_1)),
        )
        third = jnp.logical_or(corner, jnp.logical_and(right, n_right >= BATCH))
        pool = jnp.logical_not(jnp.logical_or(first, jnp.logical_or(second, third)))
        fills = jnp.logical_and(pool, n_pool < fill_2)
        mine = (
            first,
            second,
            jnp.logical_or(third, fills),
            jnp.logical_and(pool, n_pool >= fill_2),
        )[wanted]
        return mine, n_inside + one(inside), n_right + one(right), n_pool + one(pool)

    return stage


def window_kernel(wanted, ins, n_in, carried, rims, *refs):
    row_ref, col_ref, count_ref, meas, probe_ref, tables = refs[:6]
    operands = refs[6 : 6 + n_in]
    acc, *results = refs[6 + n_in + carried : -3]
    obj, wrapped, order = refs[-3:]
    capacity = meas.shape[0]
    count = count_ref[0]

    stage = plan_for(wanted, row_ref, col_ref, count)

    def pick(k, seen):
        n = seen[0]
        mine, *later = stage(k, seen[1:])
        order[n] = k
        return (n + mine.astype(jnp.int32), *later)

    zero = jnp.int32(0)
    total = lax.fori_loop(0, count, pick, (zero, zero, zero, zero))[0]

    if carried:
        acc[...] = refs[6 + n_in][...]
    else:
        acc[...] = jnp.zeros(acc.shape, F32)
    for k, outer, inner in ins:
        obj[inner] = operands[k][outer]
    for part in range(2):
        wrapped[part, pl.ds(0, 8)] = probe_ref[part, pl.ds(WIN - 8, 8)]
        wrapped[part, pl.ds(8, WIN)] = probe_ref[part]

    lane = lax.broadcasted_iota(jnp.int32, (WIN, WIN), 1)
    head_row = lax.broadcasted_iota(jnp.int32, (8, WIN), 0)

    def step(base, batch):
        slots = [order[jnp.minimum(base + k, total - 1)] for k in range(batch)]
        places = []
        for k in slots:
            row, col = row_ref[k], col_ref[k]
            top = pl.multiple_of(row // 8 * 8, 8)
            places.append((top, row - top, col // WIN, col % WIN))

        def cut(place, layer):
            top, down, col_tile, shift = place
            here = lane >= shift
            out = []
            for part in range(2):
                plane = layer * 2 + part
                body = jnp.where(
                    here, obj[plane, col_tile, pl.ds(top, WIN)], obj[plane, col_tile + 1, pl.ds(top, WIN)]
                )
                tail = jnp.where(
                    here[:8],
                    obj[plane, col_tile, pl.ds(top + WIN, 8)],
                    obj[plane, col_tile + 1, pl.ds(top + WIN, 8)],
                )
                head = jnp.where(head_row >= down, body[:8], tail)
                out.append(jnp.concatenate([head, body[8:]], axis=0))
            return tuple(out)

        def put(place, layer, grad):
            top, down, col_tile, shift = place
            here = lane >= shift
            for part in range(2):
                plane = layer * 2 + part
                value = grad[part]
                head = jnp.where(head_row >= down, value[:8], 0.0)
                tail = jnp.where(head_row < down, value[:8], 0.0)
                body = jnp.concatenate([head, value[8:]], axis=0)
                acc[plane, col_tile, pl.ds(top, WIN)] += jnp.where(here, body, 0.0)
                acc[plane, col_tile + 1, pl.ds(top, WIN)] += jnp.where(here, 0.0, body)
                acc[plane, col_tile, pl.ds(top + WIN, 8)] += jnp.where(here[:8], tail, 0.0)
                acc[plane, col_tile + 1, pl.ds(top + WIN, 8)] += jnp.where(here[:8], 0.0, tail)

        def through(items, right, left):
            out = []
            for i in range(0, batch, 2):
                out += times_left(
                    times_right(items[i : i + 2], right_table(tables, right)),
                    left_table(tables, left),
                )
            return out

        field = [
            tuple(pltpu.roll(wrapped[part, pl.ds(8 - down, WIN)], shift, 1) for part in range(2))
            for _, down, _, shift in places
        ]
        fields = []
        for layer in range(LAYERS):
            fields.append(field)
            left = [mul(f, cut(p, layer)) for f, p in zip(field, places)]
            if layer + 1 < LAYERS:
                field = through(left, PROP, PROP + 2)
        far = through(left, DFT, DFT + 2)
        grads = []
        for i, (k, (re, im)) in enumerate(zip(slots, far)):
            misfit = re * re + im * im - meas[k]
            misfit = jnp.where(base + i < total, 2.0 * misfit, 0.0)
            grads.append((misfit * re, misfit * im))
        grads = through(grads, DFT + 2, DFT)
        for layer in reversed(range(LAYERS)):
            for place, f, g in zip(places, fields[layer], grads):
                put(place, layer, mul_conj(f, g))
            if layer > 0:
                back = [mul_conj(cut(p, layer), g) for p, g in zip(places, grads)]
                grads = through(back, PROP + 2, PROP)

    small = BATCH // 2 if wanted >= 2 else 0
    rest = total % BATCH
    whole = jnp.where(rest > small, total // BATCH + 1, total // BATCH)

    @pl.loop(0, whole)
    def _(it):
        step(it * BATCH, BATCH)

    if small:

        @pl.when(jnp.logical_and(rest > 0, rest <= small))
        def _():
            step(whole * BATCH, small)

    for k, outer, inner in rims:
        results[k][outer] = acc[inner]


def per_device(object_slices, window_row, window_column, window_count, intensity, probe_wavefield):
    tile_h, tile_w = object_slices.shape[2:]
    assert tile_h == 2 * WIN and tile_w == 2 * WIN
    capacity = window_row.shape[-1]
    planes = 2 * LAYERS
    tile = object_slices.reshape(planes, tile_h, tile_w)
    rows, cols = lax.axis_size("ty"), lax.axis_size("tx")

    def along(block, axis, distance):
        devices = range(lax.axis_size(axis))
        route = [(i - distance, i) for i in devices if i - distance in devices]
        return lax.ppermute(block, axis, route)

    lower_0 = along(tile[:, :WIN, :WIN], "ty", -1)
    right = along(tile[:, :, :WIN], "tx", -1)
    lower_1 = along(tile[:, :WIN, WIN:], "ty", -1)

    common = (
        window_row.reshape(capacity),
        window_column.reshape(capacity),
        window_count.reshape(1),
        intensity.reshape(capacity, WIN, WIN),
        probe_wavefield,
        jnp.asarray(table_blocks()),
    )
    smem = pl.BlockSpec(memory_space=pltpu.SMEM)
    hbm = pl.BlockSpec(memory_space=pl.ANY)
    vmem = pl.BlockSpec(memory_space=pltpu.VMEM)
    block = (planes, WIN, WIN)
    everything = slice(None)
    high, low = slice(0, tile_h), slice(tile_h, tile_h + WIN)
    whole = (planes, 3, tile_h + WIN, WIN)

    def call(name, stage, operands, carried, ins, rims, shapes):
        kernel = functools.partial(
            window_kernel, stage, ins, len(operands), len(carried), rims
        )
        return pl.pallas_call(
            kernel,
            out_shape=[jax.ShapeDtypeStruct(s, F32) for s in (whole, *shapes)],
            in_specs=[smem] * 3 + [vmem] * (3 + len(operands) + len(carried)),
            out_specs=[vmem] * (1 + len(shapes)),
            scratch_shapes=[
                pltpu.VMEM(whole, F32),
                pltpu.VMEM((2, WIN + 8, WIN), F32),
                pltpu.SMEM((capacity + 1,), jnp.int32),
            ],
            compiler_params=pltpu.CompilerParams(vmem_limit_bytes=32 * 1024 * 1024),
            cost_estimate=pl.CostEstimate(
                flops=1_000_000, bytes_accessed=1_000_000, transcendentals=0
            ),
            name=name,
        )(*common, *operands, *carried)

    def split_cols(k):
        return [
            (k, (everything, everything, slice(t * WIN, (t + 1) * WIN)), (everything, t, high))
            for t in range(2)
        ]

    (part,) = call("inside_windows", 0, [tile], [], split_cols(0), [], [])
    lower_0, _ = lax.optimization_barrier((lower_0, part))
    corner = along(lower_0, "tx", -1)
    with_right = split_cols(0) + [(1, (everything,), (everything, 2, high))]
    (part,) = call("right_windows", 1, [tile, right, lower_0], [part], with_right, [], [])
    with_all = with_right + [(2 + t, (everything,), (everything, t, low)) for t in range(3)]
    strips = [tile, right, lower_0, lower_1, corner]
    part, right_rim, rim_corner = call(
        "corner_windows",
        2,
        strips,
        [part],
        with_all,
        [(0, (everything,), (everything, 2, high)), (1, (everything,), (everything, 2, low))],
        [(planes, tile_h, WIN), block],
    )
    corner_in = along(rim_corner, "tx", 1)
    right_in = along(right_rim, "tx", 1)
    main, rim_0, rim_1 = call(
        "lower_windows",
        3,
        strips,
        [part],
        with_all,
        [(t, (everything,), (everything, t, low)) for t in range(2)],
        [block] * 2,
    )
    lower_in_1 = along(rim_1, "ty", 1)
    lower_in_0 = along(rim_0 + corner_in, "ty", 1)

    def finish(main_ref, right_ref, low_0_ref, low_1_ref, out_ref, out, sems):
        copies = []
        for p in range(planes):
            out[p, :WIN, :WIN] = main_ref[p, 0, :WIN] + (right_ref[p, :WIN] + low_0_ref[p])
            out[p, :WIN, WIN:] = main_ref[p, 1, :WIN] + low_1_ref[p]
            out[p, WIN:, :WIN] = main_ref[p, 0, WIN:tile_h] + right_ref[p, WIN:]
            out[p, WIN:, WIN:] = main_ref[p, 1, WIN:tile_h]
            copies.append(pltpu.make_async_copy(out.at[p], out_ref.at[p], sems.at[p]))
            copies[-1].start()
        for copy in copies:
            copy.wait()

    out = pl.pallas_call(
        finish,
        out_shape=jax.ShapeDtypeStruct((planes, tile_h, tile_w), F32),
        in_specs=[vmem] * 4,
        out_specs=hbm,
        scratch_shapes=[
            pltpu.VMEM((planes, tile_h, tile_w), F32),
            pltpu.SemaphoreType.DMA((planes,)),
        ],
        compiler_params=pltpu.CompilerParams(vmem_limit_bytes=16 * 1024 * 1024),
        name="add_rims",
    )(main, right_in, lower_in_0, lower_in_1)
    return out.reshape(object_slices.shape)


def solution(mesh):
    return jax.shard_map(
        per_device,
        mesh=mesh,
        in_specs=(
            P(None, None, "ty", "tx"),
            P("ty", "tx", None),
            P("ty", "tx", None),
            P("ty", "tx"),
            P("ty", "tx", None, None, None),
            P(),
        ),
        out_specs=P(None, None, "ty", "tx"),
        check_vma=False,
    )
```

```python
import functools
import math

import jax
import jax.numpy as jnp
import ml_dtypes
import numpy as np
from jax import lax
from jax.experimental import pallas as pl
from jax.experimental.pallas import tpu as pltpu
from jax.sharding import PartitionSpec as P

WIN = 128
LAYERS = 3
BATCH = 8
PROP, DFT = 0, 4
PROPAGATE_SCALE = 60.0
F32 = jnp.float32
BF16 = jnp.bfloat16


def complex_tables():
    n = np.arange(WIN)
    dft = np.exp(-2j * math.pi * (n[:, None] * n[None, :] % WIN) / WIN) / math.sqrt(WIN)
    centred = ((n + WIN // 2) % WIN - WIN // 2) / WIN
    phase = np.exp(-1j * PROPAGATE_SCALE * centred**2)
    prop = np.conj(dft) @ (phase[:, None] * dft)
    return prop, dft


def real_form(table):
    return np.block([[table.real, table.imag], [-table.imag, table.real]])


def halves(table):
    high = table.astype(ml_dtypes.bfloat16)
    low = (table - high.astype(np.float64)).astype(ml_dtypes.bfloat16)
    return high, low


def table_blocks():
    blocks = []
    for table in complex_tables():
        for form in (real_form(table), real_form(table).T):
            blocks += halves(form)
    return np.stack(blocks)


def right_table(tables, which):
    high, low = tables[which], tables[which + 1]
    return jnp.concatenate([high, high, low], axis=0)


def left_table(tables, which):
    high, low = tables[which], tables[which + 1]
    return jnp.concatenate([high, high, low], axis=1)


def split(x):
    high = x.astype(BF16)
    low = (x - high.astype(F32)).astype(BF16)
    return high, low


def times_right(fields, table):
    rows = jnp.concatenate([jnp.concatenate(f, axis=1) for f in fields], axis=0)
    high, low = split(rows)
    out = jnp.dot(jnp.concatenate([high, low, high], axis=1), table, preferred_element_type=F32)
    return [
        (out[i * WIN : (i + 1) * WIN, :WIN], out[i * WIN : (i + 1) * WIN, WIN:])
        for i in range(len(fields))
    ]


def times_left(fields, table):
    (a_re, a_im), (b_re, b_im) = fields
    cols = jnp.concatenate(
        [jnp.concatenate([a_re, b_re], axis=1), jnp.concatenate([a_im, b_im], axis=1)], axis=0
    )
    high, low = split(cols)
    out = jnp.dot(table, jnp.concatenate([high, low, high], axis=0), preferred_element_type=F32)
    return [(out[:WIN, :WIN], out[WIN:, :WIN]), (out[:WIN, WIN:], out[WIN:, WIN:])]


def both_sides(pairs, right, left):
    return [times_left(times_right(p, right), left) for p in pairs]


def mul(a, b):
    return a[0] * b[0] - a[1] * b[1], a[0] * b[1] + a[1] * b[0]


def mul_conj(a, b):
    return a[0] * b[0] + a[1] * b[1], a[0] * b[1] - a[1] * b[0]


def plan_for(wanted, row_ref, col_ref, count):
    zero = jnp.int32(0)
    one = lambda flag: flag.astype(jnp.int32)

    def kind(k):
        low, far = row_ref[k] > WIN, col_ref[k] > WIN
        high, near = jnp.logical_not(low), jnp.logical_not(far)
        return (
            jnp.logical_and(high, near),
            jnp.logical_and(high, far),
            jnp.logical_and(low, far),
        )

    def tally(k, seen):
        return tuple(n + one(flag) for n, flag in zip(seen, kind(k)))

    n_inside_all, n_right, n_corner = lax.fori_loop(0, count, tally, (zero, zero, zero))
    small = BATCH // 2
    fill_1 = BATCH + jnp.maximum(BATCH - n_right, 0)
    n_late = n_corner + jnp.maximum(n_right - BATCH, 0)
    fill_2 = (n_late + small - 1) // small * small - n_late
    n_early = jnp.minimum(n_right, BATCH) + jnp.minimum(n_inside_all, fill_1)
    fill_2 = jnp.where(count - n_early <= BATCH + small, count, fill_2)

    def stage(k, seen):
        n_inside, n_right, n_pool = seen
        inside, right, corner = kind(k)
        first = jnp.logical_and(inside, n_inside < BATCH)
        second = jnp.logical_or(
            jnp.logical_and(right, n_right < BATCH),
            jnp.logical_and(inside, jnp.logical_and(n_inside >= BATCH, n_inside < fill_1)),
        )
        third = jnp.logical_or(corner, jnp.logical_and(right, n_right >= BATCH))
        pool = jnp.logical_not(jnp.logical_or(first, jnp.logical_or(second, third)))
        fills = jnp.logical_and(pool, n_pool < fill_2)
        mine = (
            first,
            second,
            jnp.logical_or(third, fills),
            jnp.logical_and(pool, n_pool >= fill_2),
        )[wanted]
        return mine, n_inside + one(inside), n_right + one(right), n_pool + one(pool)

    return stage


def window_kernel(wanted, ins, n_in, carried, rims, *refs):
    row_ref, col_ref, count_ref, meas, probe_ref, tables = refs[:6]
    operands = refs[6 : 6 + n_in]
    acc, *results = refs[6 + n_in + carried : -4]
    obj, wrapped, order, sems = refs[-4:]
    copies = []
    if wanted == 0:
        outer, (meas, probe_ref) = (meas, probe_ref), results
        copies = [
            pltpu.make_async_copy(src, dst, sems.at[i])
            for i, (src, dst) in enumerate(zip(outer, results))
        ]
    for copy in copies:
        copy.start()
    count = count_ref[0]

    stage = plan_for(wanted, row_ref, col_ref, count)

    def pick(k, seen):
        n = seen[0]
        mine, *later = stage(k, seen[1:])
        order[n] = k
        return (n + mine.astype(jnp.int32), *later)

    zero = jnp.int32(0)
    total = lax.fori_loop(0, count, pick, (zero, zero, zero, zero))[0]

    if carried:
        acc[...] = refs[6 + n_in][...]
    else:
        acc[...] = jnp.zeros(acc.shape, F32)
    for k, outer, inner in ins:
        obj[inner] = operands[k][outer]
    for copy in copies:
        copy.wait()
    for part in range(2):
        wrapped[part, pl.ds(0, 8)] = probe_ref[part, pl.ds(WIN - 8, 8)]
        wrapped[part, pl.ds(8, WIN)] = probe_ref[part]

    lane = lax.broadcasted_iota(jnp.int32, (WIN, WIN), 1)
    head_row = lax.broadcasted_iota(jnp.int32, (8, WIN), 0)

    def step(base, batch):
        slots = [order[jnp.minimum(base + k, total - 1)] for k in range(batch)]
        places = []
        for k in slots:
            row, col = row_ref[k], col_ref[k]
            top = pl.multiple_of(row // 8 * 8, 8)
            places.append((top, row - top, col // WIN, col % WIN))

        def cut(place, layer):
            top, down, col_tile, shift = place
            here = lane >= shift
            out = []
            for part in range(2):
                plane = layer * 2 + part
                body = jnp.where(
                    here, obj[plane, col_tile, pl.ds(top, WIN)], obj[plane, col_tile + 1, pl.ds(top, WIN)]
                )
                tail = jnp.where(
                    here[:8],
                    obj[plane, col_tile, pl.ds(top + WIN, 8)],
                    obj[plane, col_tile + 1, pl.ds(top + WIN, 8)],
                )
                head = jnp.where(head_row >= down, body[:8], tail)
                out.append(jnp.concatenate([head, body[8:]], axis=0))
            return tuple(out)

        def put(place, layer, grad):
            top, down, col_tile, shift = place
            here = lane >= shift
            for part in range(2):
                plane = layer * 2 + part
                value = grad[part]
                head = jnp.where(head_row >= down, value[:8], 0.0)
                tail = jnp.where(head_row < down, value[:8], 0.0)
                body = jnp.concatenate([head, value[8:]], axis=0)
                acc[plane, col_tile, pl.ds(top, WIN)] += jnp.where(here, body, 0.0)
                acc[plane, col_tile + 1, pl.ds(top, WIN)] += jnp.where(here, 0.0, body)
                acc[plane, col_tile, pl.ds(top + WIN, 8)] += jnp.where(here[:8], tail, 0.0)
                acc[plane, col_tile + 1, pl.ds(top + WIN, 8)] += jnp.where(here[:8], 0.0, tail)

        def through(items, right, left):
            out = []
            for i in range(0, batch, 2):
                out += times_left(
                    times_right(items[i : i + 2], right_table(tables, right)),
                    left_table(tables, left),
                )
            return out

        field = [
            tuple(pltpu.roll(wrapped[part, pl.ds(8 - down, WIN)], shift, 1) for part in range(2))
            for _, down, _, shift in places
        ]
        fields = []
        for layer in range(LAYERS):
            fields.append(field)
            left = [mul(f, cut(p, layer)) for f, p in zip(field, places)]
            if layer + 1 < LAYERS:
                field = through(left, PROP, PROP + 2)
        far = through(left, DFT, DFT + 2)
        grads = []
        for i, (k, (re, im)) in enumerate(zip(slots, far)):
            misfit = re * re + im * im - meas[k]
            misfit = jnp.where(base + i < total, 2.0 * misfit, 0.0)
            grads.append((misfit * re, misfit * im))
        grads = through(grads, DFT + 2, DFT)
        for layer in reversed(range(LAYERS)):
            for place, f, g in zip(places, fields[layer], grads):
                put(place, layer, mul_conj(f, g))
            if layer > 0:
                back = [mul_conj(cut(p, layer), g) for p, g in zip(places, grads)]
                grads = through(back, PROP + 2, PROP)

    small = BATCH // 2 if wanted >= 2 else 0
    rest = total % BATCH
    whole = jnp.where(rest > small, total // BATCH + 1, total // BATCH)

    @pl.loop(0, whole)
    def _(it):
        step(it * BATCH, BATCH)

    if small:

        @pl.when(jnp.logical_and(rest > 0, rest <= small))
        def _():
            step(whole * BATCH, small)

    for k, outer, inner in rims:
        results[k][outer] = acc[inner]


def per_device(object_slices, window_row, window_column, window_count, intensity, probe_wavefield):
    tile_h, tile_w = object_slices.shape[2:]
    assert tile_h == 2 * WIN and tile_w == 2 * WIN
    capacity = window_row.shape[-1]
    planes = 2 * LAYERS
    tile = object_slices.reshape(planes, tile_h, tile_w)
    rows, cols = lax.axis_size("ty"), lax.axis_size("tx")

    def along(block, axis, distance):
        devices = range(lax.axis_size(axis))
        route = [(i - distance, i) for i in devices if i - distance in devices]
        return lax.ppermute(block, axis, route)

    lower_0 = along(tile[:, :WIN, :WIN], "ty", -1)
    right = along(tile[:, :, :WIN], "tx", -1)
    lower_1 = along(tile[:, :WIN, WIN:], "ty", -1)

    common = (
        window_row.reshape(capacity),
        window_column.reshape(capacity),
        window_count.reshape(1),
        intensity.reshape(capacity, WIN, WIN),
        probe_wavefield,
        jnp.asarray(table_blocks()),
    )
    smem = pl.BlockSpec(memory_space=pltpu.SMEM)
    hbm = pl.BlockSpec(memory_space=pl.ANY)
    vmem = pl.BlockSpec(memory_space=pltpu.VMEM)
    block = (planes, WIN, WIN)
    everything = slice(None)
    high, low = slice(0, tile_h), slice(tile_h, tile_h + WIN)
    whole = (planes, 3, tile_h + WIN, WIN)

    def call(name, stage, operands, carried, ins, rims, shapes, common):
        kernel = functools.partial(
            window_kernel, stage, ins, len(operands), len(carried), rims
        )
        return pl.pallas_call(
            kernel,
            out_shape=[jax.ShapeDtypeStruct(s, F32) for s in (whole, *shapes)],
            in_specs=[smem] * 3
            + [hbm if stage == 0 else vmem] * 2
            + [vmem] * (1 + len(operands) + len(carried)),
            out_specs=[vmem] * (1 + len(shapes)),
            scratch_shapes=[
                pltpu.VMEM(whole, F32),
                pltpu.VMEM((2, WIN + 8, WIN), F32),
                pltpu.SMEM((capacity + 1,), jnp.int32),
                pltpu.SemaphoreType.DMA((2,)),
            ],
            compiler_params=pltpu.CompilerParams(vmem_limit_bytes=32 * 1024 * 1024),
            cost_estimate=pl.CostEstimate(
                flops=10_000_000, bytes_accessed=1, transcendentals=0
            ),
            name=name,
        )(*common, *operands, *carried)

    def split_cols(k):
        return [
            (k, (everything, everything, slice(t * WIN, (t + 1) * WIN)), (everything, t, high))
            for t in range(2)
        ]

    fetched = [common[3].shape, common[4].shape]
    part, *held = call("inside_windows", 0, [tile], [], split_cols(0), [], fetched, common)
    common = (*common[:3], *held, common[5])
    lower_0, _ = lax.optimization_barrier((lower_0, part))
    corner = along(lower_0, "tx", -1)
    with_right = split_cols(0) + [(1, (everything,), (everything, 2, high))]
    (part,) = call("right_windows", 1, [tile, right, lower_0], [part], with_right, [], [], common)
    with_all = with_right + [(2 + t, (everything,), (everything, t, low)) for t in range(3)]
    strips = [tile, right, lower_0, lower_1, corner]
    part, right_rim, rim_corner = call(
        "corner_windows",
        2,
        strips,
        [part],
        with_all,
        [(0, (everything,), (everything, 2, high)), (1, (everything,), (everything, 2, low))],
        [(planes, tile_h, WIN), block],
        common,
    )
    corner_in = along(rim_corner, "tx", 1)
    right_in = along(right_rim, "tx", 1)
    main, rim_0, rim_1 = call(
        "lower_windows",
        3,
        strips,
        [part],
        with_all,
        [(t, (everything,), (everything, t, low)) for t in range(2)],
        [block] * 2,
        common,
    )
    lower_in_1 = along(rim_1, "ty", 1)
    lower_in_0 = along(rim_0 + corner_in, "ty", 1)

    def finish(main_ref, right_ref, low_0_ref, low_1_ref, out_ref, out, sems):
        copies = []
        for p in range(planes):
            out[p, :WIN, :WIN] = main_ref[p, 0, :WIN] + (right_ref[p, :WIN] + low_0_ref[p])
            out[p, :WIN, WIN:] = main_ref[p, 1, :WIN] + low_1_ref[p]
            out[p, WIN:, :WIN] = main_ref[p, 0, WIN:tile_h] + right_ref[p, WIN:]
            out[p, WIN:, WIN:] = main_ref[p, 1, WIN:tile_h]
            copies.append(pltpu.make_async_copy(out.at[p], out_ref.at[p], sems.at[p]))
            copies[-1].start()
        for copy in copies:
            copy.wait()

    out = pl.pallas_call(
        finish,
        out_shape=jax.ShapeDtypeStruct((planes, tile_h, tile_w), F32),
        in_specs=[vmem] * 4,
        out_specs=hbm,
        scratch_shapes=[
            pltpu.VMEM((planes, tile_h, tile_w), F32),
            pltpu.SemaphoreType.DMA((planes,)),
        ],
        compiler_params=pltpu.CompilerParams(vmem_limit_bytes=16 * 1024 * 1024),
        name="add_rims",
    )(main, right_in, lower_in_0, lower_in_1)
    return out.reshape(object_slices.shape)


def solution(mesh):
    return jax.shard_map(
        per_device,
        mesh=mesh,
        in_specs=(
            P(None, None, "ty", "tx"),
            P("ty", "tx", None),
            P("ty", "tx", None),
            P("ty", "tx"),
            P("ty", "tx", None, None, None),
            P(),
        ),
        out_specs=P(None, None, "ty", "tx"),
        check_vma=False,
    )
```

```python
import functools
import math

import jax
import jax.numpy as jnp
import ml_dtypes
import numpy as np
from jax import lax
from jax.experimental import pallas as pl
from jax.experimental.pallas import tpu as pltpu
from jax.sharding import PartitionSpec as P

WIN = 128
LAYERS = 3
BATCH = 8
PROP, DFT = 0, 4
PROPAGATE_SCALE = 60.0
F32 = jnp.float32
BF16 = jnp.bfloat16


def complex_tables():
    n = np.arange(WIN)
    dft = np.exp(-2j * math.pi * (n[:, None] * n[None, :] % WIN) / WIN) / math.sqrt(WIN)
    centred = ((n + WIN // 2) % WIN - WIN // 2) / WIN
    phase = np.exp(-1j * PROPAGATE_SCALE * centred**2)
    prop = np.conj(dft) @ (phase[:, None] * dft)
    return prop, dft


def real_form(table):
    return np.block([[table.real, table.imag], [-table.imag, table.real]])


def halves(table):
    high = table.astype(ml_dtypes.bfloat16)
    low = (table - high.astype(np.float64)).astype(ml_dtypes.bfloat16)
    return high, low


def table_blocks():
    blocks = []
    for table in complex_tables():
        for form in (real_form(table), real_form(table).T):
            blocks += halves(form)
    return np.stack(blocks)


def right_table(tables, which):
    high, low = tables[which], tables[which + 1]
    return jnp.concatenate([high, high, low], axis=0)


def left_table(tables, which):
    high, low = tables[which], tables[which + 1]
    return jnp.concatenate([high, high, low], axis=1)


def split(x):
    high = x.astype(BF16)
    low = (x - high.astype(F32)).astype(BF16)
    return high, low


def times_right(fields, table):
    rows = jnp.concatenate([jnp.concatenate(f, axis=1) for f in fields], axis=0)
    high, low = split(rows)
    out = jnp.dot(jnp.concatenate([high, low, high], axis=1), table, preferred_element_type=F32)
    return [
        (out[i * WIN : (i + 1) * WIN, :WIN], out[i * WIN : (i + 1) * WIN, WIN:])
        for i in range(len(fields))
    ]


def times_left(fields, table):
    (a_re, a_im), (b_re, b_im) = fields
    cols = jnp.concatenate(
        [jnp.concatenate([a_re, b_re], axis=1), jnp.concatenate([a_im, b_im], axis=1)], axis=0
    )
    high, low = split(cols)
    out = jnp.dot(table, jnp.concatenate([high, low, high], axis=0), preferred_element_type=F32)
    return [(out[:WIN, :WIN], out[WIN:, :WIN]), (out[:WIN, WIN:], out[WIN:, WIN:])]


def both_sides(pairs, right, left):
    return [times_left(times_right(p, right), left) for p in pairs]


def mul(a, b):
    return a[0] * b[0] - a[1] * b[1], a[0] * b[1] + a[1] * b[0]


def mul_conj(a, b):
    return a[0] * b[0] + a[1] * b[1], a[0] * b[1] - a[1] * b[0]


def plan_for(wanted, row_ref, col_ref, count):
    zero = jnp.int32(0)
    one = lambda flag: flag.astype(jnp.int32)

    def kind(k):
        low, far = row_ref[k] > WIN, col_ref[k] > WIN
        high, near = jnp.logical_not(low), jnp.logical_not(far)
        return (
            jnp.logical_and(high, near),
            jnp.logical_and(high, far),
            jnp.logical_and(low, far),
        )

    def tally(k, seen):
        return tuple(n + one(flag) for n, flag in zip(seen, kind(k)))

    n_inside_all, n_right, n_corner = lax.fori_loop(0, count, tally, (zero, zero, zero))
    small = BATCH // 2
    fill_1 = BATCH + jnp.maximum(BATCH - n_right, 0)
    n_late = n_corner + jnp.maximum(n_right - BATCH, 0)
    fill_2 = (n_late + small - 1) // small * small - n_late
    n_early = jnp.minimum(n_right, BATCH) + jnp.minimum(n_inside_all, fill_1)
    fill_2 = jnp.where(count - n_early <= BATCH + small, count, fill_2)

    def stage(k, seen):
        n_inside, n_right, n_pool = seen
        inside, right, corner = kind(k)
        first = jnp.logical_and(inside, n_inside < BATCH)
        second = jnp.logical_or(
            jnp.logical_and(right, n_right < BATCH),
            jnp.logical_and(inside, jnp.logical_and(n_inside >= BATCH, n_inside < fill_1)),
        )
        third = jnp.logical_or(corner, jnp.logical_and(right, n_right >= BATCH))
        pool = jnp.logical_not(jnp.logical_or(first, jnp.logical_or(second, third)))
        fills = jnp.logical_and(pool, n_pool < fill_2)
        mine = (
            first,
            second,
            jnp.logical_or(third, fills),
            jnp.logical_and(pool, n_pool >= fill_2),
        )[wanted]
        return mine, n_inside + one(inside), n_right + one(right), n_pool + one(pool)

    return stage


def window_kernel(wanted, ins, n_in, carried, rims, *refs):
    row_ref, col_ref, count_ref, meas, probe_ref, tables = refs[:6]
    operands = refs[6 : 6 + n_in]
    acc, *results = refs[6 + n_in + carried : -4]
    obj, wrapped, order, sems = refs[-4:]
    copies = []
    if wanted == 0:
        outer, (meas, probe_ref) = (meas, probe_ref), results
        copies = [
            pltpu.make_async_copy(src, dst, sems.at[i])
            for i, (src, dst) in enumerate(zip(outer, results))
        ]
    for copy in copies:
        copy.start()
    count = count_ref[0]

    stage = plan_for(wanted, row_ref, col_ref, count)

    def pick(k, seen):
        n = seen[0]
        mine, *later = stage(k, seen[1:])
        order[n] = k
        return (n + mine.astype(jnp.int32), *later)

    zero = jnp.int32(0)
    total = lax.fori_loop(0, count, pick, (zero, zero, zero, zero))[0]

    if carried:
        acc[...] = refs[6 + n_in][...]
    else:
        acc[...] = jnp.zeros(acc.shape, F32)
    for k, outer, inner in ins:
        obj[inner] = operands[k][outer]
    for copy in copies:
        copy.wait()
    for part in range(2):
        wrapped[part, pl.ds(0, 8)] = probe_ref[part, pl.ds(WIN - 8, 8)]
        wrapped[part, pl.ds(8, WIN)] = probe_ref[part]

    lane = lax.broadcasted_iota(jnp.int32, (WIN, WIN), 1)
    head_row = lax.broadcasted_iota(jnp.int32, (8, WIN), 0)

    def step(base, batch):
        slots = [order[jnp.minimum(base + k, total - 1)] for k in range(batch)]
        places = []
        for k in slots:
            row, col = row_ref[k], col_ref[k]
            top = pl.multiple_of(row // 8 * 8, 8)
            places.append((top, row - top, col // WIN, col % WIN))

        def cut(place, layer):
            top, down, col_tile, shift = place
            here = lane >= shift
            out = []
            for part in range(2):
                plane = layer * 2 + part
                body = jnp.where(
                    here, obj[plane, col_tile, pl.ds(top, WIN)], obj[plane, col_tile + 1, pl.ds(top, WIN)]
                )
                tail = jnp.where(
                    here[:8],
                    obj[plane, col_tile, pl.ds(top + WIN, 8)],
                    obj[plane, col_tile + 1, pl.ds(top + WIN, 8)],
                )
                head = jnp.where(head_row >= down, body[:8], tail)
                out.append(jnp.concatenate([head, body[8:]], axis=0))
            return tuple(out)

        def put(place, layer, grad):
            top, down, col_tile, shift = place
            here = lane >= shift
            for part in range(2):
                plane = layer * 2 + part
                value = grad[part]
                head = jnp.where(head_row >= down, value[:8], 0.0)
                tail = jnp.where(head_row < down, value[:8], 0.0)
                body = jnp.concatenate([head, value[8:]], axis=0)
                acc[plane, col_tile, pl.ds(top, WIN)] += jnp.where(here, body, 0.0)
                acc[plane, col_tile + 1, pl.ds(top, WIN)] += jnp.where(here, 0.0, body)
                acc[plane, col_tile, pl.ds(top + WIN, 8)] += jnp.where(here[:8], tail, 0.0)
                acc[plane, col_tile + 1, pl.ds(top + WIN, 8)] += jnp.where(here[:8], 0.0, tail)

        def through(items, right, left):
            out = []
            for i in range(0, batch, 2):
                out += times_left(
                    times_right(items[i : i + 2], right_table(tables, right)),
                    left_table(tables, left),
                )
            return out

        field = [
            tuple(pltpu.roll(wrapped[part, pl.ds(8 - down, WIN)], shift, 1) for part in range(2))
            for _, down, _, shift in places
        ]
        fields = []
        for layer in range(LAYERS):
            fields.append(field)
            left = [mul(f, cut(p, layer)) for f, p in zip(field, places)]
            if layer + 1 < LAYERS:
                field = through(left, PROP, PROP + 2)
        far = through(left, DFT, DFT + 2)
        grads = []
        for i, (k, (re, im)) in enumerate(zip(slots, far)):
            misfit = re * re + im * im - meas[k]
            misfit = jnp.where(base + i < total, 2.0 * misfit, 0.0)
            grads.append((misfit * re, misfit * im))
        grads = through(grads, DFT + 2, DFT)
        for layer in reversed(range(LAYERS)):
            for place, f, g in zip(places, fields[layer], grads):
                put(place, layer, mul_conj(f, g))
            if layer > 0:
                back = [mul_conj(cut(p, layer), g) for p, g in zip(places, grads)]
                grads = through(back, PROP + 2, PROP)

    small = BATCH // 2 if wanted >= 2 else 0
    rest = total % BATCH
    whole = jnp.where(rest > small, total // BATCH + 1, total // BATCH)

    @pl.loop(0, whole)
    def _(it):
        step(it * BATCH, BATCH)

    if small:

        @pl.when(jnp.logical_and(rest > 0, rest <= small))
        def _():
            step(whole * BATCH, small)

    for k, outer, inner in rims:
        results[k][outer] = acc[inner]


def per_device(object_slices, window_row, window_column, window_count, intensity, probe_wavefield):
    tile_h, tile_w = object_slices.shape[2:]
    assert tile_h == 2 * WIN and tile_w == 2 * WIN
    capacity = window_row.shape[-1]
    planes = 2 * LAYERS
    tile = object_slices.reshape(planes, tile_h, tile_w)
    rows, cols = lax.axis_size("ty"), lax.axis_size("tx")

    def along(block, axis, distance):
        devices = range(lax.axis_size(axis))
        route = [(i - distance, i) for i in devices if i - distance in devices]
        return lax.ppermute(block, axis, route)

    lower_0 = along(tile[:, :WIN, :WIN], "ty", -1)
    right = along(tile[:, :, :WIN], "tx", -1)
    lower_1 = along(tile[:, :WIN, WIN:], "ty", -1)

    common = (
        window_row.reshape(capacity),
        window_column.reshape(capacity),
        window_count.reshape(1),
        intensity.reshape(capacity, WIN, WIN),
        probe_wavefield,
        jnp.asarray(table_blocks()),
    )
    smem = pl.BlockSpec(memory_space=pltpu.SMEM)
    hbm = pl.BlockSpec(memory_space=pl.ANY)
    vmem = pl.BlockSpec(memory_space=pltpu.VMEM)
    block = (planes, WIN, WIN)
    everything = slice(None)
    high, low = slice(0, tile_h), slice(tile_h, tile_h + WIN)
    whole = (planes, 3, tile_h + WIN, WIN)

    def call(name, stage, operands, carried, ins, rims, shapes, common):
        kernel = functools.partial(
            window_kernel, stage, ins, len(operands), len(carried), rims
        )
        return pl.pallas_call(
            kernel,
            out_shape=[jax.ShapeDtypeStruct(s, F32) for s in (whole, *shapes)],
            in_specs=[smem] * 3
            + [hbm if stage == 0 else vmem] * 2
            + [vmem] * (1 + len(operands) + len(carried)),
            out_specs=[vmem] * (1 + len(shapes)),
            scratch_shapes=[
                pltpu.VMEM(whole, F32),
                pltpu.VMEM((2, WIN + 8, WIN), F32),
                pltpu.SMEM((capacity + 1,), jnp.int32),
                pltpu.SemaphoreType.DMA((2,)),
            ],
            compiler_params=pltpu.CompilerParams(vmem_limit_bytes=32 * 1024 * 1024),
            cost_estimate=pl.CostEstimate(
                flops=10_000_000, bytes_accessed=1, transcendentals=0
            ),
            name=name,
        )(*common, *operands, *carried)

    def split_cols(k):
        return [
            (k, (everything, everything, slice(t * WIN, (t + 1) * WIN)), (everything, t, high))
            for t in range(2)
        ]

    fetched = [common[3].shape, common[4].shape]
    part, *held = call("inside_windows", 0, [tile], [], split_cols(0), [], fetched, common)
    common = (*common[:3], *held, common[5])
    lower_0, _ = lax.optimization_barrier((lower_0, part))
    corner = along(lower_0, "tx", -1)
    with_right = split_cols(0) + [(1, (everything,), (everything, 2, high))]
    (part,) = call("right_windows", 1, [tile, right, lower_0], [part], with_right, [], [], common)
    with_all = with_right + [(2 + t, (everything,), (everything, t, low)) for t in range(3)]
    strips = [tile, right, lower_0, lower_1, corner]
    part, right_rim = call(
        "corner_windows",
        2,
        strips,
        [part],
        with_all,
        [(0, (everything,), (everything, 2))],
        [(planes, tile_h + WIN, WIN)],
        common,
    )
    right_in = along(right_rim, "tx", 1)
    main, rim_0, rim_1 = call(
        "lower_windows",
        3,
        strips,
        [part],
        with_all,
        [(t, (everything,), (everything, t, low)) for t in range(2)],
        [block] * 2,
        common,
    )
    lower_in_1 = along(rim_1, "ty", 1)
    lower_in_0 = along(rim_0 + right_in[:, tile_h:], "ty", 1)

    def finish(main_ref, right_ref, low_0_ref, low_1_ref, out_ref, out, sems):
        copies = []
        for p in range(planes):
            out[p, :WIN, :WIN] = main_ref[p, 0, :WIN] + (right_ref[p, :WIN] + low_0_ref[p])
            out[p, :WIN, WIN:] = main_ref[p, 1, :WIN] + low_1_ref[p]
            out[p, WIN:, :WIN] = main_ref[p, 0, WIN:tile_h] + right_ref[p, WIN:tile_h]
            out[p, WIN:, WIN:] = main_ref[p, 1, WIN:tile_h]
            copies.append(pltpu.make_async_copy(out.at[p], out_ref.at[p], sems.at[p]))
            copies[-1].start()
        for copy in copies:
            copy.wait()

    out = pl.pallas_call(
        finish,
        out_shape=jax.ShapeDtypeStruct((planes, tile_h, tile_w), F32),
        in_specs=[vmem] * 4,
        out_specs=hbm,
        scratch_shapes=[
            pltpu.VMEM((planes, tile_h, tile_w), F32),
            pltpu.SemaphoreType.DMA((planes,)),
        ],
        compiler_params=pltpu.CompilerParams(vmem_limit_bytes=16 * 1024 * 1024),
        name="add_rims",
    )(main, right_in, lower_in_0, lower_in_1)
    return out.reshape(object_slices.shape)


def solution(mesh):
    return jax.shard_map(
        per_device,
        mesh=mesh,
        in_specs=(
            P(None, None, "ty", "tx"),
            P("ty", "tx", None),
            P("ty", "tx", None),
            P("ty", "tx"),
            P("ty", "tx", None, None, None),
            P(),
        ),
        out_specs=P(None, None, "ty", "tx"),
        check_vma=False,
    )
```

```python
import functools
import math

import jax
import jax.numpy as jnp
import ml_dtypes
import numpy as np
from jax import lax
from jax.experimental import pallas as pl
from jax.experimental.pallas import tpu as pltpu
from jax.sharding import PartitionSpec as P

WIN = 128
LAYERS = 3
BATCH = 8
PROP, DFT = 0, 4
PROPAGATE_SCALE = 60.0
F32 = jnp.float32
BF16 = jnp.bfloat16


def complex_tables():
    n = np.arange(WIN)
    dft = np.exp(-2j * math.pi * (n[:, None] * n[None, :] % WIN) / WIN) / math.sqrt(WIN)
    centred = ((n + WIN // 2) % WIN - WIN // 2) / WIN
    phase = np.exp(-1j * PROPAGATE_SCALE * centred**2)
    prop = np.conj(dft) @ (phase[:, None] * dft)
    return prop, dft


def real_form(table):
    return np.block([[table.real, table.imag], [-table.imag, table.real]])


def halves(table):
    high = table.astype(ml_dtypes.bfloat16)
    low = (table - high.astype(np.float64)).astype(ml_dtypes.bfloat16)
    return high, low


def table_blocks():
    blocks = []
    for table in complex_tables():
        for form in (real_form(table), real_form(table).T):
            blocks += halves(form)
    return np.stack(blocks)


def right_table(tables, which):
    high, low = tables[which], tables[which + 1]
    return jnp.concatenate([high, high, low], axis=0)


def left_table(tables, which):
    high, low = tables[which], tables[which + 1]
    return jnp.concatenate([high, high, low], axis=1)


def split(x):
    high = x.astype(BF16)
    low = (x - high.astype(F32)).astype(BF16)
    return high, low


def times_right(fields, table):
    rows = jnp.concatenate([jnp.concatenate(f, axis=1) for f in fields], axis=0)
    high, low = split(rows)
    out = jnp.dot(jnp.concatenate([high, low, high], axis=1), table, preferred_element_type=F32)
    return [
        (out[i * WIN : (i + 1) * WIN, :WIN], out[i * WIN : (i + 1) * WIN, WIN:])
        for i in range(len(fields))
    ]


def times_left(fields, table):
    (a_re, a_im), (b_re, b_im) = fields
    cols = jnp.concatenate(
        [jnp.concatenate([a_re, b_re], axis=1), jnp.concatenate([a_im, b_im], axis=1)], axis=0
    )
    high, low = split(cols)
    out = jnp.dot(table, jnp.concatenate([high, low, high], axis=0), preferred_element_type=F32)
    return [(out[:WIN, :WIN], out[WIN:, :WIN]), (out[:WIN, WIN:], out[WIN:, WIN:])]


def both_sides(pairs, right, left):
    return [times_left(times_right(p, right), left) for p in pairs]


def mul(a, b):
    return a[0] * b[0] - a[1] * b[1], a[0] * b[1] + a[1] * b[0]


def mul_conj(a, b):
    return a[0] * b[0] + a[1] * b[1], a[0] * b[1] - a[1] * b[0]


def plan_for(wanted, row_ref, col_ref, count):
    zero = jnp.int32(0)
    one = lambda flag: flag.astype(jnp.int32)

    def kind(k):
        low, far = row_ref[k] > WIN, col_ref[k] > WIN
        high, near = jnp.logical_not(low), jnp.logical_not(far)
        return (
            jnp.logical_and(high, near),
            jnp.logical_and(high, far),
            jnp.logical_and(low, far),
        )

    def tally(k, seen):
        return tuple(n + one(flag) for n, flag in zip(seen, kind(k)))

    n_inside_all, n_right, n_corner = lax.fori_loop(0, count, tally, (zero, zero, zero))
    small = BATCH // 2
    fill_1 = BATCH + jnp.maximum(BATCH - n_right, 0)
    n_late = n_corner + jnp.maximum(n_right - BATCH, 0)
    fill_2 = (n_late + small - 1) // small * small - n_late
    n_early = jnp.minimum(n_right, BATCH) + jnp.minimum(n_inside_all, fill_1)
    fill_2 = jnp.where(count - n_early <= BATCH + small, count, fill_2)

    def stage(k, seen):
        n_inside, n_right, n_pool = seen
        inside, right, corner = kind(k)
        first = jnp.logical_and(inside, n_inside < BATCH)
        second = jnp.logical_or(
            jnp.logical_and(right, n_right < BATCH),
            jnp.logical_and(inside, jnp.logical_and(n_inside >= BATCH, n_inside < fill_1)),
        )
        third = jnp.logical_or(corner, jnp.logical_and(right, n_right >= BATCH))
        pool = jnp.logical_not(jnp.logical_or(first, jnp.logical_or(second, third)))
        fills = jnp.logical_and(pool, n_pool < fill_2)
        mine = (
            first,
            second,
            jnp.logical_or(third, fills),
            jnp.logical_and(pool, n_pool >= fill_2),
        )[wanted]
        return mine, n_inside + one(inside), n_right + one(right), n_pool + one(pool)

    return stage


def window_kernel(wanted, ins, n_in, carried, rims, *refs):
    row_ref, col_ref, count_ref, meas, probe_ref, tables = refs[:6]
    operands = refs[6 : 6 + n_in]
    acc, *results = refs[6 + n_in + carried : -4]
    obj, wrapped, order, sems = refs[-4:]
    copies = []
    if wanted == 0:
        outer, (meas, probe_ref) = (meas, probe_ref), results
        copies = [
            pltpu.make_async_copy(src, dst, sems.at[i])
            for i, (src, dst) in enumerate(zip(outer, results))
        ]
    for copy in copies:
        copy.start()
    count = count_ref[0]

    stage = plan_for(wanted, row_ref, col_ref, count)

    def pick(k, seen):
        n = seen[0]
        mine, *later = stage(k, seen[1:])
        order[n] = k
        return (n + mine.astype(jnp.int32), *later)

    zero = jnp.int32(0)
    total = lax.fori_loop(0, count, pick, (zero, zero, zero, zero))[0]

    if not carried:
        acc[...] = jnp.zeros(acc.shape, F32)
    for k, outer, inner in ins:
        obj[inner] = operands[k][outer]
    for copy in copies:
        copy.wait()
    for part in range(2):
        wrapped[part, pl.ds(0, 8)] = probe_ref[part, pl.ds(WIN - 8, 8)]
        wrapped[part, pl.ds(8, WIN)] = probe_ref[part]

    lane = lax.broadcasted_iota(jnp.int32, (WIN, WIN), 1)
    head_row = lax.broadcasted_iota(jnp.int32, (8, WIN), 0)

    def step(base, batch):
        slots = [order[jnp.minimum(base + k, total - 1)] for k in range(batch)]
        places = []
        for k in slots:
            row, col = row_ref[k], col_ref[k]
            top = pl.multiple_of(row // 8 * 8, 8)
            places.append((top, row - top, col // WIN, col % WIN))

        def cut(place, layer):
            top, down, col_tile, shift = place
            here = lane >= shift
            out = []
            for part in range(2):
                plane = layer * 2 + part
                body = jnp.where(
                    here, obj[plane, col_tile, pl.ds(top, WIN)], obj[plane, col_tile + 1, pl.ds(top, WIN)]
                )
                tail = jnp.where(
                    here[:8],
                    obj[plane, col_tile, pl.ds(top + WIN, 8)],
                    obj[plane, col_tile + 1, pl.ds(top + WIN, 8)],
                )
                head = jnp.where(head_row >= down, body[:8], tail)
                out.append(jnp.concatenate([head, body[8:]], axis=0))
            return tuple(out)

        def put(place, layer, grad):
            top, down, col_tile, shift = place
            here = lane >= shift
            for part in range(2):
                plane = layer * 2 + part
                value = grad[part]
                head = jnp.where(head_row >= down, value[:8], 0.0)
                tail = jnp.where(head_row < down, value[:8], 0.0)
                body = jnp.concatenate([head, value[8:]], axis=0)
                acc[plane, col_tile, pl.ds(top, WIN)] += jnp.where(here, body, 0.0)
                acc[plane, col_tile + 1, pl.ds(top, WIN)] += jnp.where(here, 0.0, body)
                acc[plane, col_tile, pl.ds(top + WIN, 8)] += jnp.where(here[:8], tail, 0.0)
                acc[plane, col_tile + 1, pl.ds(top + WIN, 8)] += jnp.where(here[:8], 0.0, tail)

        def through(items, right, left):
            out = []
            for i in range(0, batch, 2):
                out += times_left(
                    times_right(items[i : i + 2], right_table(tables, right)),
                    left_table(tables, left),
                )
            return out

        field = [
            tuple(pltpu.roll(wrapped[part, pl.ds(8 - down, WIN)], shift, 1) for part in range(2))
            for _, down, _, shift in places
        ]
        fields = []
        for layer in range(LAYERS):
            fields.append(field)
            left = [mul(f, cut(p, layer)) for f, p in zip(field, places)]
            if layer + 1 < LAYERS:
                field = through(left, PROP, PROP + 2)
        far = through(left, DFT, DFT + 2)
        grads = []
        for i, (k, (re, im)) in enumerate(zip(slots, far)):
            misfit = re * re + im * im - meas[k]
            misfit = jnp.where(base + i < total, 2.0 * misfit, 0.0)
            grads.append((misfit * re, misfit * im))
        grads = through(grads, DFT + 2, DFT)
        for layer in reversed(range(LAYERS)):
            for place, f, g in zip(places, fields[layer], grads):
                put(place, layer, mul_conj(f, g))
            if layer > 0:
                back = [mul_conj(cut(p, layer), g) for p, g in zip(places, grads)]
                grads = through(back, PROP + 2, PROP)

    small = BATCH // 2 if wanted >= 2 else 0
    rest = total % BATCH
    whole = jnp.where(rest > small, total // BATCH + 1, total // BATCH)

    @pl.loop(0, whole)
    def _(it):
        step(it * BATCH, BATCH)

    if small:

        @pl.when(jnp.logical_and(rest > 0, rest <= small))
        def _():
            step(whole * BATCH, small)

    for k, outer, inner in rims:
        results[k][outer] = acc[inner]


def per_device(object_slices, window_row, window_column, window_count, intensity, probe_wavefield):
    tile_h, tile_w = object_slices.shape[2:]
    assert tile_h == 2 * WIN and tile_w == 2 * WIN
    capacity = window_row.shape[-1]
    planes = 2 * LAYERS
    tile = object_slices.reshape(planes, tile_h, tile_w)
    rows, cols = lax.axis_size("ty"), lax.axis_size("tx")

    def along(block, axis, distance):
        devices = range(lax.axis_size(axis))
        route = [(i - distance, i) for i in devices if i - distance in devices]
        return lax.ppermute(block, axis, route)

    lower_0 = along(tile[:, :WIN, :WIN], "ty", -1)
    right = along(tile[:, :, :WIN], "tx", -1)
    lower_1 = along(tile[:, :WIN, WIN:], "ty", -1)

    common = (
        window_row.reshape(capacity),
        window_column.reshape(capacity),
        window_count.reshape(1),
        intensity.reshape(capacity, WIN, WIN),
        probe_wavefield,
        jnp.asarray(table_blocks()),
    )
    smem = pl.BlockSpec(memory_space=pltpu.SMEM)
    hbm = pl.BlockSpec(memory_space=pl.ANY)
    vmem = pl.BlockSpec(memory_space=pltpu.VMEM)
    block = (planes, WIN, WIN)
    everything = slice(None)
    high, low = slice(0, tile_h), slice(tile_h, tile_h + WIN)
    whole = (planes, 3, tile_h + WIN, WIN)

    def call(name, stage, operands, carried, ins, rims, shapes, common):
        kernel = functools.partial(
            window_kernel, stage, ins, len(operands), len(carried), rims
        )
        return pl.pallas_call(
            kernel,
            out_shape=[jax.ShapeDtypeStruct(s, F32) for s in (whole, *shapes)],
            in_specs=[smem] * 3
            + [hbm if stage == 0 else vmem] * 2
            + [vmem] * (1 + len(operands) + len(carried)),
            out_specs=[vmem] * (1 + len(shapes)),
            scratch_shapes=[
                pltpu.VMEM(whole, F32),
                pltpu.VMEM((2, WIN + 8, WIN), F32),
                pltpu.SMEM((capacity + 1,), jnp.int32),
                pltpu.SemaphoreType.DMA((2,)),
            ],
            input_output_aliases={6 + len(operands): 0} if carried else {},
            compiler_params=pltpu.CompilerParams(vmem_limit_bytes=32 * 1024 * 1024),
            cost_estimate=pl.CostEstimate(
                flops=10_000_000, bytes_accessed=1, transcendentals=0
            ),
            name=name,
        )(*common, *operands, *carried)

    def split_cols(k):
        return [
            (k, (everything, everything, slice(t * WIN, (t + 1) * WIN)), (everything, t, high))
            for t in range(2)
        ]

    fetched = [common[3].shape, common[4].shape]
    part, *held = call("inside_windows", 0, [tile], [], split_cols(0), [], fetched, common)
    common = (*common[:3], *held, common[5])
    lower_0, _ = lax.optimization_barrier((lower_0, part))
    corner = along(lower_0, "tx", -1)
    with_right = split_cols(0) + [(1, (everything,), (everything, 2, high))]
    (part,) = call("right_windows", 1, [tile, right, lower_0], [part], with_right, [], [], common)
    with_all = with_right + [(2 + t, (everything,), (everything, t, low)) for t in range(3)]
    strips = [tile, right, lower_0, lower_1, corner]
    part, right_rim = call(
        "corner_windows",
        2,
        strips,
        [part],
        with_all,
        [(0, (everything,), (everything, 2))],
        [(planes, tile_h + WIN, WIN)],
        common,
    )
    right_in = along(right_rim, "tx", 1)
    main, rim_0, rim_1 = call(
        "lower_windows",
        3,
        strips,
        [part],
        with_all,
        [(t, (everything,), (everything, t, low)) for t in range(2)],
        [block] * 2,
        common,
    )
    lower_in_1 = along(rim_1, "ty", 1)
    lower_in_0 = along(rim_0 + right_in[:, tile_h:], "ty", 1)

    def finish(main_ref, right_ref, low_0_ref, low_1_ref, out_ref, out, sems):
        copies = []
        for p in range(planes):
            out[p, :WIN, :WIN] = main_ref[p, 0, :WIN] + (right_ref[p, :WIN] + low_0_ref[p])
            out[p, :WIN, WIN:] = main_ref[p, 1, :WIN] + low_1_ref[p]
            out[p, WIN:, :WIN] = main_ref[p, 0, WIN:tile_h] + right_ref[p, WIN:tile_h]
            out[p, WIN:, WIN:] = main_ref[p, 1, WIN:tile_h]
            copies.append(pltpu.make_async_copy(out.at[p], out_ref.at[p], sems.at[p]))
            copies[-1].start()
        for copy in copies:
            copy.wait()

    out = pl.pallas_call(
        finish,
        out_shape=jax.ShapeDtypeStruct((planes, tile_h, tile_w), F32),
        in_specs=[vmem] * 4,
        out_specs=hbm,
        scratch_shapes=[
            pltpu.VMEM((planes, tile_h, tile_w), F32),
            pltpu.SemaphoreType.DMA((planes,)),
        ],
        compiler_params=pltpu.CompilerParams(vmem_limit_bytes=16 * 1024 * 1024),
        name="add_rims",
    )(main, right_in, lower_in_0, lower_in_1)
    return out.reshape(object_slices.shape)


def solution(mesh):
    return jax.shard_map(
        per_device,
        mesh=mesh,
        in_specs=(
            P(None, None, "ty", "tx"),
            P("ty", "tx", None),
            P("ty", "tx", None),
            P("ty", "tx"),
            P("ty", "tx", None, None, None),
            P(),
        ),
        out_specs=P(None, None, "ty", "tx"),
        check_vma=False,
    )
```
